256 devices in a mesh: batch: 2 (over x_hi), seq: 8 (over z), pool: 16 (over y, x_lo, core).
Axes of the slice: x: 4 (x_hi: 2, x_lo: 2; x = x_hi * 2 + x_lo), y: 4, z: 8, core: 2. Of those that a mesh axis runs over, the one named last changes fastest.
Arguments:
- tokens: bfloat16 [32, 2048, 1024], P(('batch', 'pool'), 'seq'), may hold values from -6 to 6
- w_in: bfloat16 [1024, 4096], replicated, may hold values from -0.1875 to 0.1875
- w_out: bfloat16 [1024, 1024], replicated, may hold values from -0.1875 to 0.1875
- w_proj: bfloat16 [1024, 256], replicated, may hold values from -0.1875 to 0.1875
- pos_embed: bfloat16 [32, 2048, 256], P(('batch', 'pool'), 'seq'), may hold values from -6 to 6
- pos_ids: int32 [32, 2048], P(('batch', 'pool'), 'seq'), may hold values from 0 to 1048575
- lengths: int32 [32], P(('batch', 'pool')), may hold values from 256 to 2048, as said below
- neg_embed: bfloat16 [2, 4096, 256], P('batch', 'pool'), may hold values from -0.375 to 0.375
- neg_ids: int32 [2, 4096], P('batch', 'pool'), may hold values from 0 to 1048575
Outputs:
- loss: float32 [32, 2048], P(('batch', 'pool'), 'seq')
- d_neg: float32 [2, 4096, 256], P('batch', 'pool', 'seq')
- d_proj: float32 [1024, 256], replicated
The draws below stay inside these ranges and needn't reach their ends.
Inputs may be any that keep to these rules, and one draw needn't show every extreme that they name: `lengths`: every history has at least one valid event; in every draw one history is valid over all 2048 events.
All inputs are finite; a program needn't handle non-finite values.
Results may differ from the reference program's by a relative error of at most 0.017.
Values may be sent and summed in bfloat16 or wider, within the bound.
A program may use at most 128 MiB of HBM per device.

```python
import math
import jax
import jax.numpy as jnp
import numpy as np
from jax import lax

D = 1024
HEADS = 8
E = 256
NEG = 4096
ITEMS = 1048576
LEN = 2048
HIST = 32
N_BATCH = 2
N_POOL = 16


def draw_lengths(key, part):
    key = jax.random.fold_in(key, 11)
    key_len, key_top = jax.random.split(key)
    drawn = jax.random.randint(key_len, (HIST,), LEN // 8, LEN + 1)
    chosen = jax.random.randint(key_top, (), 0, HIST)
    return jnp.where(jnp.arange(HIST) == chosen, LEN, drawn).astype(jnp.int32)


def touch_ends(values, rng, smallest, largest):
    longest = values.shape.index(max(values.shape))
    spots = []
    for shift in (0, 1):
        where = [jax.random.randint(jax.random.fold_in(rng, axis), (), 0, length) for axis, length in enumerate(values.shape)]
        where[longest] = (where[longest] + shift) % values.shape[longest]
        spots.append(tuple(where))
    return values.at[spots[0]].set(smallest).at[spots[1]].set(largest)


def block_scale(key, shape, cuts, smallest, high):
    gain, own = 1.0, jax.random.fold_in(key, 6)
    for position, shards_of in cuts:
        draws = jnp.exp(jax.random.uniform(jax.random.fold_in(own, position), (shards_of,), jnp.float32, smallest / len(cuts), high / len(cuts)))
        gain = gain * jnp.repeat(draws, shape[position] // shards_of).reshape([-1 if axis == position else 1 for axis in range(len(shape))])
    return gain


def skewed_wide(rng, shape, amount, skew):
    loads = [min(1 << octave, amount + 1 - (1 << octave)) * (1 << 20) // math.isqrt((1 << octave) ** skew) + 1 for octave in range((amount + 1).bit_length()) if 1 << octave <= amount]
    scale = 1 + sum(loads) // (1 << 30)
    grid = np.cumsum(np.array([max(1, weight // scale) for weight in loads]))
    lot = jax.random.randint(jax.random.fold_in(rng, 1), shape, 0, int(grid[len(loads) - 1]))
    start = jnp.left_shift(1, jnp.searchsorted(jnp.asarray(grid, jnp.int32), lot, side="right").astype(jnp.int32))
    grade = start - 1 + jax.random.randint(jax.random.fold_in(rng, 4), shape, 0, 1 << 30) % jnp.minimum(start, amount + 1 - start)
    return jax.random.permutation(jax.random.fold_in(rng, 2), amount)[grade].astype(jnp.int32)


def normal_values(own_key, dims, deviation, reach, cuts=(), kind=jnp.bfloat16):
    gain = block_scale(own_key, dims, cuts, -0.22, 0.18) if cuts else 1.0
    entries = jax.random.normal(own_key, dims, jnp.float32) * deviation * gain
    return jnp.minimum(jnp.maximum(entries, -reach), reach).astype(kind)


def setup_inputs(seed: int = 0) -> dict:
    arg_keys = jax.random.split(jax.random.key(seed), 10)
    return {
        "tokens": normal_values(arg_keys[0], (HIST, LEN, D), 1.0, 6.0, ((0, 32), (1, 8))),
        "w_in": normal_values(arg_keys[1], (D, 4 * D), D ** -0.5, 0.1875),
        "w_out": normal_values(arg_keys[2], (D, D), D ** -0.5, 0.1875),
        "w_proj": normal_values(arg_keys[3], (D, E), D ** -0.5, 0.1875),
        "pos_embed": normal_values(arg_keys[4], (HIST, LEN, E), 1.0, 6.0, ((0, 32), (1, 8))),
        "pos_ids": touch_ends(skewed_wide(arg_keys[5], (HIST, LEN), ITEMS, 2), jax.random.fold_in(arg_keys[5], 3), 0, ITEMS - 1).astype(jnp.int32),
        "lengths": draw_lengths(jax.random.fold_in(arg_keys[9], 71), 0),
        "neg_embed": normal_values(arg_keys[7], (N_BATCH, NEG, E), E ** -0.5, 0.375, ((0, 2), (1, 16))),
        "neg_ids": touch_ends(skewed_wide(arg_keys[8], (N_BATCH, NEG), ITEMS, 2), jax.random.fold_in(arg_keys[8], 3), 0, ITEMS - 1).astype(jnp.int32),
    }


SOFTMAX_WARMTH = 0.02
NORM_EPSILON = 1e-05
UNIT_EPSILON = 1e-06

def layer_norm(inputs):
    center = inputs - lax.optimization_barrier(jnp.mean(inputs, axis=-1, keepdims=True))
    spread = lax.optimization_barrier(jnp.mean(center * center, axis=-1, keepdims=True))
    return center / jnp.sqrt(spread + NORM_EPSILON)

def unit_rows(inputs):
    norms = jnp.sqrt(lax.optimization_barrier(jnp.sum(inputs * inputs, axis=-1, keepdims=True)) + UNIT_EPSILON)
    return (inputs / norms, norms)

def log_sample_chance(item_ids):
    ranks = item_ids.astype(jnp.float32) + 1.0
    return jnp.log(jnp.log1p(1.0 / ranks)) - jnp.log(jnp.log(jnp.float32(ITEMS) + 1.0))

def head_split(block):
    return block.reshape(block.shape[0], HEADS, block.shape[1] // HEADS).transpose(1, 0, 2)

def attend(query_block, query_pos, key_block, value_block, key_pos, length):
    width = query_block.shape[1]
    head_width = width // HEADS
    allowed = (key_pos[None, :] <= query_pos[:, None]) & (key_pos[None, :] < length)

    def one_head(parts):
        query_head, key_head, value_head = parts
        scores = jnp.dot(query_head, key_head.T, preferred_element_type=jnp.float32) / math.sqrt(head_width)
        weights = jnp.where(allowed, jax.nn.silu(scores), 0.0).astype(jnp.bfloat16)
        return jnp.dot(weights, value_head, preferred_element_type=jnp.float32)
    result = lax.map(one_head, (head_split(query_block), head_split(key_block), head_split(value_block)))
    return result.transpose(1, 0, 2).reshape(query_block.shape[0], width)

def reference(tokens, w_in, w_out, w_proj, pos_embed, pos_ids, lengths, neg_embed, neg_ids):
    unit_negs, neg_norms = unit_rows(neg_embed.astype(jnp.float32))
    negative_estimate = unit_negs.astype(jnp.bfloat16)
    positions = jnp.arange(LEN, dtype=jnp.int32)
    groups = jnp.arange(HIST, dtype=jnp.int32) // N_POOL

    def per_history(parts):
        history, pos_rows, positive_targets, length, group = parts
        width = history.shape[1]
        normed = layer_norm(history.astype(jnp.float32)).astype(jnp.bfloat16)
        mixed = jax.nn.silu(jnp.dot(normed, w_in, preferred_element_type=jnp.float32))
        gate_u = mixed[:, :width].astype(jnp.bfloat16)
        values = mixed[:, width:2 * width].astype(jnp.bfloat16)
        queries = mixed[:, 2 * width:3 * width].astype(jnp.bfloat16)
        keys = mixed[:, 3 * width:].astype(jnp.bfloat16)
        attn = attend(queries, positions, keys, values, positions, length)
        gated = (layer_norm(attn) * gate_u.astype(jnp.float32)).astype(jnp.bfloat16)
        layer_out = (jnp.dot(gated, w_out, preferred_element_type=jnp.float32) + history.astype(jnp.float32)).astype(jnp.bfloat16)
        out_unit, out_norms = unit_rows(jnp.dot(layer_out, w_proj, preferred_element_type=jnp.float32))
        output_estimate = out_unit.astype(jnp.bfloat16)
        positive_direction = unit_rows(pos_rows.astype(jnp.float32))[0]
        valid = positions < length
        group_estimate = negative_estimate[group]
        group_labels = neg_ids[group]
        positive_score = lax.optimization_barrier(jnp.sum(output_estimate.astype(jnp.float32) * positive_direction, axis=-1)) / SOFTMAX_WARMTH - log_sample_chance(positive_targets)
        negative_score = jnp.dot(output_estimate, group_estimate.T, preferred_element_type=jnp.float32) / SOFTMAX_WARMTH - log_sample_chance(group_labels)[None, :]
        kept = jnp.where(group_labels[None, :] != positive_targets[:, None], jnp.exp(negative_score), 0.0)
        total = jnp.exp(positive_score) + lax.optimization_barrier(jnp.sum(kept, axis=-1))
        loss = jnp.where(valid, jnp.log(total) - positive_score, 0.0)
        negative_weights = (jnp.where(valid[:, None], kept / total[:, None], 0.0) / HIST).astype(jnp.bfloat16)
        positive_weight = jnp.where(valid, jnp.exp(positive_score) / total - 1.0, 0.0) / HIST
        negative_portion = jnp.dot(negative_weights.T, output_estimate, preferred_element_type=jnp.float32) / SOFTMAX_WARMTH
        unit_gradient = (positive_weight[:, None] * positive_direction + jnp.dot(negative_weights, group_estimate, preferred_element_type=jnp.float32)) / SOFTMAX_WARMTH
        d_out = ((unit_gradient - out_unit * lax.optimization_barrier(jnp.sum(out_unit * unit_gradient, axis=-1, keepdims=True))) / out_norms).astype(jnp.bfloat16)
        proj_part = jnp.dot(layer_out.T, d_out, preferred_element_type=jnp.float32)
        return (loss, negative_portion, proj_part)
    loss, neg_parts, proj_parts = lax.map(per_history, (tokens, pos_embed, pos_ids, lengths, groups))
    neg_sum = lax.optimization_barrier(jnp.sum(neg_parts.reshape(N_BATCH, N_POOL, NEG, E), axis=1))
    d_neg = (neg_sum - unit_negs * lax.optimization_barrier(jnp.sum(unit_negs * neg_sum, axis=-1, keepdims=True))) / neg_norms
    d_proj = lax.optimization_barrier(jnp.sum(proj_parts, axis=0))
    return (loss, d_neg, d_proj)
```

```python
import math

import jax
import jax.numpy as jnp
from jax import lax
from jax.experimental import pallas as pl
from jax.experimental.pallas import tpu as pltpu
from jax.sharding import PartitionSpec as P

HEADS = 8
HEAD = 128
ROWS = 256
WIDTH = 1024
EMBED = 256
SEQ = 8
POOL = 16
BATCH = 2
GRID = 16
ITEMS = 1048576
HIST = 32
WARMTH = 0.02
NORM_EPSILON = 1e-05
UNIT_EPSILON = 1e-06
MESH = pl.DeviceIdType.MESH
F32 = jnp.float32
BF16 = jnp.bfloat16


def dot(a, b):
    return jnp.dot(a, b, preferred_element_type=F32)


def dot_nt(a, b):
    return lax.dot_general(a, b, (((1,), (1,)), ((), ())), preferred_element_type=F32)


def dot_tn(a, b):
    return lax.dot_general(a, b, (((0,), (0,)), ((), ())), preferred_element_type=F32)


def silu(v):
    half = 0.5 * v
    return half + half * jnp.tanh(half)


def layer_norm(inputs):
    center = inputs - jnp.mean(inputs, axis=-1, keepdims=True)
    spread = jnp.mean(center * center, axis=-1, keepdims=True)
    return center * lax.rsqrt(spread + NORM_EPSILON)


def inverse_chance(ids):
    z = 1.0 / (2.0 * ids + 3.0)
    z2 = z * z
    series = 1.0 / 17.0
    for odd in (15, 13, 11, 9, 7, 5, 3, 1):
        series = series * z2 + 1.0 / odd
    return math.log(ITEMS + 1.0) / (2.0 * z * series)


def far_first(i):
    return 4 + (1 - 2 * (i % 2)) * ((i + 1) // 2)


def remote(src, dst, send, recv, **device):
    return pltpu.make_async_remote_copy(
        src_ref=src, dst_ref=dst, send_sem=send, recv_sem=recv, device_id=device, device_id_type=MESH
    )


def kernel(
    tokens,
    w_in,
    w_out,
    w_proj,
    pos_embed,
    pos_ids,
    lengths,
    neg_embed,
    neg_ids,
    loss_ref,
    dneg_ref,
    dproj_ref,
    wkv,
    wq,
    wg,
    wo,
    wp,
    normed,
    kvs,
    kvr,
    qs,
    qr,
    osend,
    orecv,
    gate,
    negs,
    negs_t,
    ids_all,
    cmask,
    kept,
    pos_t,
    cs,
    cr,
    own,
    xs,
    xr,
    ys,
    yr,
    zs,
    zr,
    pcs,
    pcr,
    pown,
    pzs,
    pzr,
    pxr,
    fin,
    w_sem,
    kv_sem,
    q_sem,
    o_sem,
    neg_sem,
    id_sem,
    c_sem,
    x_sem,
    y_sem,
    z_sem,
    pc_sem,
    pz_sem,
    px_sem,
    f_sem,
    fc_sem,
):
    b = lax.axis_index("batch")
    s = lax.axis_index("seq")
    p = lax.axis_index("pool")
    core = p % 2
    xlo = (p // 2) % 2
    y = p // 4
    sibling = p + 1 - 2 * core
    across = p + 2 - 4 * xlo
    q_own = b * 8 + p // 2

    def load_kv(k):
        h = (s + k) % SEQ
        return [
            pltpu.make_async_copy(
                w_in.at[:, pl.ds(pl.multiple_of(3 * WIDTH + h * HEAD, HEAD), HEAD)],
                wkv.at[k, :, pl.ds(0, HEAD)],
                w_sem.at[k],
            ),
            pltpu.make_async_copy(
                w_in.at[:, pl.ds(pl.multiple_of(WIDTH + h * HEAD, HEAD), HEAD)],
                wkv.at[k, :, pl.ds(HEAD, HEAD)],
                w_sem.at[8 + k],
            ),
        ]

    def load_q(i, half):
        h = (s + far_first(2 * i + half)) % SEQ
        return pltpu.make_async_copy(
            w_in.at[:, pl.ds(pl.multiple_of(2 * WIDTH + h * HEAD, HEAD), HEAD)],
            wq.at[i, :, pl.ds(half * HEAD, HEAD)],
            w_sem.at[16 + 2 * i + half],
        )

    load_g = pltpu.make_async_copy(w_in.at[:, pl.ds(0, WIDTH)], wg, w_sem.at[24])
    load_o = pltpu.make_async_copy(w_out, wo, w_sem.at[25])
    load_p = pltpu.make_async_copy(w_proj, wp, w_sem.at[26])
    for i in range(8):
        for c in load_kv(far_first(i)):
            c.start()
    for i in range(4):
        load_q(i, 0).start()
        load_q(i, 1).start()
    load_g.start()
    load_o.start()
    load_p.start()

    barrier = pltpu.get_barrier_semaphore()

    @pl.loop(1, SEQ)
    def _(k):
        pl.semaphore_signal(barrier, inc=1, device_id={"seq": (s + k) % SEQ}, device_id_type=MESH)

    @pl.loop(1, POOL)
    def _(k):
        pl.semaphore_signal(barrier, inc=1, device_id={"pool": (p + k) % POOL}, device_id_type=MESH)

    @pl.loop(0, POOL // 2)
    def _(k):
        pl.semaphore_signal(
            barrier, inc=1, device_id={"batch": 1 - b, "pool": 2 * k + core}, device_id_type=MESH
        )

    @pl.loop(0, 4)
    def _(i):
        rows = pl.ds(pl.multiple_of(i * 64, 64), 64)
        normed[rows, :] = layer_norm(tokens[rows, :].astype(F32)).astype(BF16)

    length = lengths[0]
    row_pos = s * ROWS + lax.broadcasted_iota(jnp.int32, (ROWS, 1), 0)
    row_valid = row_pos < length

    pl.semaphore_wait(barrier, (SEQ - 1) + (POOL - 1) + POOL // 2)

    def send_kv(k):
        return remote(
            kvs.at[k], kvr.at[s], kv_sem.at[0, k], kv_sem.at[1, k], seq=(s + k) % SEQ
        )

    def recv_kv(k):
        return remote(
            kvs.at[k], kvr.at[(s + SEQ - k) % SEQ], kv_sem.at[0, k], kv_sem.at[1, k], seq=(s + k) % SEQ
        )

    @pl.loop(0, SEQ)
    def _(i):
        k = far_first(i)
        for c in load_kv(k):
            c.wait()
        both = silu(dot(normed[...], wkv[k]))
        keys = both[:, :HEAD].astype(BF16)
        values = jnp.where(row_valid, both[:, HEAD:], 0.0).astype(BF16)

        @pl.when(i < SEQ - 1)
        def _():
            kvs[k, 0] = keys
            kvs[k, 1] = values
            send_kv(k).start()

        @pl.when(i == SEQ - 1)
        def _():
            kvr[s, 0] = keys
            kvr[s, 1] = values

    def send_q(k):
        return remote(qs.at[k], qr.at[s], q_sem.at[0, k], q_sem.at[1, k], seq=(s + k) % SEQ)

    def recv_q(k):
        return remote(
            qs.at[k], qr.at[(s + SEQ - k) % SEQ], q_sem.at[0, k], q_sem.at[1, k], seq=(s + k) % SEQ
        )

    @pl.loop(0, SEQ // 2)
    def _(i):
        load_q(i, 0).wait()
        load_q(i, 1).wait()
        both = silu(dot(normed[...], wq[i])).astype(BF16)
        k0 = far_first(2 * i)
        k1 = far_first(2 * i + 1)
        qs[k0] = both[:, :HEAD]
        send_q(k0).start()

        @pl.when(i < SEQ // 2 - 1)
        def _():
            qs[k1] = both[:, HEAD:]
            send_q(k1).start()

        @pl.when(i == SEQ // 2 - 1)
        def _():
            qr[s] = both[:, HEAD:]

    neg = neg_embed[...].astype(F32)
    neg_norm = jnp.sqrt(jnp.sum(neg * neg, axis=-1, keepdims=True) + UNIT_EPSILON)
    negs[p] = (neg / neg_norm).astype(BF16)
    ids_all[p] = neg_ids[...]

    def send_ids(k):
        return remote(ids_all.at[p], ids_all.at[p], id_sem.at[0, k], id_sem.at[1, k], pool=(p + k) % POOL)

    def recv_ids(k):
        src = (p + POOL - k) % POOL
        return remote(ids_all.at[src], ids_all.at[src], id_sem.at[0, k], id_sem.at[1, k], pool=src)

    def send_negs(k):
        return remote(negs.at[p], negs.at[p], neg_sem.at[0, k], neg_sem.at[1, k], pool=(p + k) % POOL)

    def recv_negs(k):
        src = (p + POOL - k) % POOL
        return remote(negs.at[src], negs.at[src], neg_sem.at[0, k], neg_sem.at[1, k], pool=src)

    @pl.loop(1, POOL)
    def _(k):
        send_ids(k).start()

    @pl.loop(1, POOL)
    def _(k):
        send_negs(k).start()

    load_g.wait()

    @pl.loop(0, 4)
    def _(i):
        cols = pl.ds(pl.multiple_of(i * 256, 256), 256)
        gate[:, cols] = silu(dot(normed[...], wg[:, cols])).astype(BF16)

    pos = jnp.transpose(pos_embed[...].astype(F32))
    pos_t[...] = pos / jnp.sqrt(jnp.sum(pos * pos, axis=0, keepdims=True) + UNIT_EPSILON)
    pos_row = pos_ids[...]

    @pl.loop(1, POOL)
    def _(k):
        recv_ids(k).wait_recv()

    ids = jnp.concatenate([ids_all[j] for j in range(POOL)], axis=0)
    factor = jnp.transpose(inverse_chance(ids.astype(F32)))
    ids_col = jnp.transpose(ids.astype(F32)).astype(jnp.int32)
    for j in range(POOL):
        cmask[j] = jnp.where(ids_col[:, j : j + 1] != pos_row, factor[:, j : j + 1], 0.0)

    def send_o(k):
        dst = (s + SEQ - k) % SEQ
        return remote(osend.at[k], orecv.at[s], o_sem.at[0, k], o_sem.at[1, k], seq=dst)

    def recv_o(k):
        src = (s + k) % SEQ
        return remote(osend.at[k], orecv.at[src], o_sem.at[0, k], o_sem.at[1, k], seq=src)

    @pl.loop(1, SEQ)
    def _(k):
        recv_kv(k).wait_recv()

    scale = 0.5 / math.sqrt(HEAD)

    @pl.loop(0, SEQ)
    def _(i):
        k = far_first((i + SEQ - 1) % SEQ)
        a = (s + SEQ - k) % SEQ

        @pl.when(i > 0)
        def _():
            recv_q(k).wait_recv()

        query = qr[a]

        def weights(u):
            half = scale * dot_nt(query, kvr[u, 0])
            return half + half * jnp.tanh(half)

        def group(g, total):
            return (
                total
                + dot(weights(2 * g).astype(BF16), kvr[2 * g, 1])
                + dot(weights(2 * g + 1).astype(BF16), kvr[2 * g + 1, 1])
            )

        total = lax.fori_loop(0, a // 2, group, jnp.zeros((ROWS, HEAD), F32))
        last = 2 * (a // 2)
        t_pos = a * ROWS + lax.broadcasted_iota(jnp.int32, (ROWS, ROWS), 0)
        u_pos = lax.broadcasted_iota(jnp.int32, (ROWS, ROWS), 1)
        for u in (last, last + 1):
            seen = jnp.where(u * ROWS + u_pos <= t_pos, weights(u), 0.0).astype(BF16)
            total = total + dot(seen, kvr[u, 1])

        @pl.when(i > 0)
        def _():
            osend[k] = total.astype(BF16)
            send_o(k).start()

        @pl.when(i == 0)
        def _():
            orecv[s] = total.astype(BF16)

    @pl.loop(0, POOL)
    def _(k):
        @pl.when(k > 0)
        def _():
            recv_negs(k).wait_recv()

        src = (p + POOL - k) % POOL
        negs_t[src] = jnp.transpose(negs[src])

    load_o.wait()
    load_p.wait()

    @pl.loop(1, SEQ)
    def _(k):
        recv_o(k).wait_recv()

    attn = jnp.concatenate([orecv[h] for h in range(HEADS)], axis=1).astype(F32)
    gated = (layer_norm(attn) * gate[...].astype(F32)).astype(BF16)
    layer_out = (dot(gated, wo[...]) + tokens[...].astype(F32)).astype(BF16)
    out = dot(layer_out, wp[...])
    out_hat = (out * lax.rsqrt(jnp.sum(out * out, axis=-1, keepdims=True) + UNIT_EPSILON)).astype(BF16)
    out_t = jnp.transpose(out)
    norm_t = jnp.sqrt(jnp.sum(out_t * out_t, axis=0, keepdims=True) + UNIT_EPSILON)
    unit_t = out_t / norm_t
    hat_t = unit_t.astype(BF16)
    pos_dot = jnp.sum(hat_t.astype(F32) * pos_t[...], axis=0, keepdims=True) * (1.0 / WARMTH)
    pos_chance = inverse_chance(pos_row.astype(F32))
    pos_logit = pos_dot + jnp.log(pos_chance)
    pos_exp = jnp.exp(pos_logit)

    def scores(j, total):
        value = jnp.exp(dot(negs[j], hat_t) * (1.0 / WARMTH)) * cmask[j]
        kept[j] = value
        return total + jnp.sum(value, axis=0, keepdims=True)

    total = lax.fori_loop(0, POOL, scores, jnp.zeros((1, ROWS), F32)) + pos_exp
    valid = s * ROWS + lax.broadcasted_iota(jnp.int32, (1, ROWS), 1) < length
    loss_ref[...] = jnp.where(valid, jnp.log(total) - pos_logit, 0.0)
    share = jnp.where(valid, 1.0 / (total * HIST), 0.0)
    pos_weight = jnp.where(valid, pos_exp / total - 1.0, 0.0) * (1.0 / HIST)

    def send_c(m):
        return remote(cs.at[m], cr.at[m], c_sem.at[0, m], c_sem.at[1, m], pool=sibling)

    def other_core(m, rows_t):
        j = 2 * m + 1 - core
        weight = (kept[j] * share).astype(BF16)
        cs[m] = (dot(weight, out_hat) * (1.0 / WARMTH)).astype(BF16)
        send_c(m).start()
        return rows_t + dot(negs_t[j], weight)

    def this_core(m, rows_t):
        j = 2 * m + core
        weight = (kept[j] * share).astype(BF16)
        own[m] = dot(weight, out_hat) * (1.0 / WARMTH)
        return rows_t + dot(negs_t[j], weight)

    rows_t = lax.fori_loop(0, 8, other_core, jnp.zeros((EMBED, ROWS), F32))
    rows_t = lax.fori_loop(0, 8, this_core, rows_t)

    grad_t = (pos_weight * pos_t[...] + rows_t) * (1.0 / WARMTH)
    d_out = jnp.transpose(
        (grad_t - unit_t * jnp.sum(unit_t * grad_t, axis=0, keepdims=True)) / norm_t
    ).astype(BF16)
    term = dot_tn(layer_out, d_out)
    half_rows = WIDTH // 2

    for c in range(2):
        part = term[c * half_rows : (c + 1) * half_rows]

        @pl.when(core == c)
        def _():
            pown[...] = part

        @pl.when(core != c)
        def _():
            pcs[...] = part.astype(BF16)

    send_pc = remote(pcs, pcr, pc_sem.at[0], pc_sem.at[1], pool=sibling)
    send_pc.start()

    def send_x(i):
        return remote(xs.at[i], xr.at[i], x_sem.at[0, i], x_sem.at[1, i], pool=across)

    @pl.loop(0, 4)
    def _(i):
        m = 2 * i + 1 - xlo
        send_c(m).wait_recv()
        xs[i] = (own[m] + cr[m].astype(F32)).astype(BF16)
        send_x(i).start()

    def send_pz(k):
        return remote(
            pzs.at[k], pzr.at[k], pz_sem.at[0, k], pz_sem.at[1, k], seq=(s + k) % SEQ
        )

    send_pc.wait_recv()

    @pl.loop(1, SEQ)
    def _(k):
        rows = pl.ds(pl.multiple_of(((s + k) % SEQ) * 64, 64), 64)
        pzs[k] = (pown[rows, :] + pcr[rows, :].astype(F32)).astype(BF16)
        send_pz(k).start()

    own_rows = pl.ds(pl.multiple_of(s * 64, 64), 64)
    block = pown[own_rows, :] + pcr[own_rows, :].astype(F32)

    def send_y(k):
        return remote(
            ys.at[k], yr.at[k], y_sem.at[0, k], y_sem.at[1, k], pool=((y + k) % 4) * 4 + p % 4
        )

    @pl.loop(0, 4)
    def _(i):
        m = 2 * i + xlo
        send_c(m).wait_recv()
        own[m] = own[m] + cr[m].astype(F32)

    @pl.loop(1, 4)
    def _(k):
        i = (y + k) % 4
        m = 2 * i + xlo
        send_x(i).wait_recv()
        ys[k] = (own[m] + xr[i].astype(F32)).astype(BF16)
        send_y(k).start()

    send_x(y).wait_recv()
    neg_sum = own[2 * y + xlo] + xr[y].astype(F32)

    def send_px(k):
        q = (q_own + k) % GRID
        return remote(
            pxr.at[q_own],
            pxr.at[q_own],
            px_sem.at[0, k],
            px_sem.at[1, k],
            batch=q // 8,
            pool=2 * (q % 8) + core,
        )

    def recv_px(k):
        q = (q_own + GRID - k) % GRID
        return remote(
            pxr.at[q], pxr.at[q], px_sem.at[0, k], px_sem.at[1, k], batch=q // 8, pool=2 * (q % 8) + core
        )

    for k in range(1, SEQ):
        send_pz(k).wait_recv()
        block = block + pzr[k].astype(F32)
    pxr[q_own] = block.astype(BF16)

    @pl.loop(1, GRID)
    def _(k):
        send_px(k).start()

    def send_z(k):
        return remote(zs.at[k], zr.at[k], z_sem.at[0, k], z_sem.at[1, k], seq=(s + k) % SEQ)

    for k in range(1, 4):
        send_y(k).wait_recv()
        neg_sum = neg_sum + yr[k].astype(F32)
    neg = neg_embed[...].astype(F32)
    neg_norm = jnp.sqrt(jnp.sum(neg * neg, axis=-1, keepdims=True) + UNIT_EPSILON)
    neg_unit = neg / neg_norm
    neg_term = (neg_sum - neg_unit * jnp.sum(neg_unit * neg_sum, axis=-1, keepdims=True)) / neg_norm
    cr_t = jnp.transpose(neg_term)
    own[0] = cr_t

    @pl.loop(1, SEQ)
    def _(k):
        rows = pl.ds(pl.multiple_of(((s + k) % SEQ) * 32, 32), 32)
        zs[k] = own[0, rows, :].astype(BF16)
        send_z(k).start()

    @pl.loop(1, GRID)
    def _(k):
        recv_px(k).wait_recv()

    whole = pxr[0].astype(F32)
    for q in range(1, GRID):
        whole = whole + pxr[q].astype(F32)
    fin[core * SEQ + s] = whole.astype(BF16)

    def send_f(k):
        at = core * SEQ + s
        return remote(fin.at[at], fin.at[at], f_sem.at[0, k], f_sem.at[1, k], seq=(s + k) % SEQ)

    def recv_f(k):
        at = core * SEQ + (s + SEQ - k) % SEQ
        return remote(fin.at[at], fin.at[at], f_sem.at[0, k], f_sem.at[1, k], seq=(s + k) % SEQ)

    def send_fc(k):
        at = core * SEQ + (s + SEQ - k) % SEQ
        return remote(fin.at[at], fin.at[at], fc_sem.at[0, k], fc_sem.at[1, k], pool=sibling)

    def recv_fc(k):
        at = (1 - core) * SEQ + (s + SEQ - k) % SEQ
        return remote(fin.at[at], fin.at[at], fc_sem.at[0, k], fc_sem.at[1, k], pool=sibling)

    @pl.loop(1, SEQ)
    def _(k):
        send_f(k).start()

    send_fc(0).start()

    part = own[0, pl.ds(pl.multiple_of(s * 32, 32), 32), :]
    for k in range(1, SEQ):
        send_z(k).wait_recv()
        part = part + zr[k].astype(F32)
    dneg_ref[...] = jnp.transpose(part)

    @pl.loop(1, SEQ)
    def _(k):
        recv_f(k).wait_recv()
        send_fc(k).start()

    @pl.loop(0, SEQ)
    def _(k):
        recv_fc(k).wait_recv()

    @pl.loop(0, 16)
    def _(i):
        dproj_ref[pl.ds(pl.multiple_of(i * 64, 64), 64), :] = fin[i].astype(F32)

    @pl.loop(1, SEQ)
    def _(k):
        send_kv(k).wait_send()
        send_q(k).wait_send()
        send_o(k).wait_send()
        send_pz(k).wait_send()
        send_z(k).wait_send()
        send_f(k).wait_send()

    @pl.loop(1, POOL)
    def _(k):
        send_ids(k).wait_send()
        send_negs(k).wait_send()
        send_px(k).wait_send()

    @pl.loop(0, 8)
    def _(m):
        send_c(m).wait_send()
        send_fc(m).wait_send()

    @pl.loop(0, 4)
    def _(i):
        send_x(i).wait_send()

    @pl.loop(1, 4)
    def _(k):
        send_y(k).wait_send()

    send_pc.wait_send()


def body(tokens, w_in, w_out, w_proj, pos_embed, pos_ids, lengths, neg_embed, neg_ids):
    vmem = pl.BlockSpec(memory_space=pltpu.VMEM)
    hbm = pl.BlockSpec(memory_space=pl.ANY)
    smem = pl.BlockSpec(memory_space=pltpu.SMEM)
    dma = pltpu.SemaphoreType.DMA
    loss, d_neg, d_proj = pl.pallas_call(
        kernel,
        out_shape=(
            jax.ShapeDtypeStruct((1, ROWS), F32),
            jax.ShapeDtypeStruct((ROWS, EMBED // SEQ), F32),
            jax.ShapeDtypeStruct((WIDTH, EMBED), F32),
        ),
        in_specs=[vmem, hbm, hbm, hbm, vmem, vmem, smem, vmem, vmem],
        out_specs=(vmem, vmem, vmem),
        scratch_shapes=[
            pltpu.VMEM((8, WIDTH, 256), BF16),
            pltpu.VMEM((4, WIDTH, 256), BF16),
            pltpu.VMEM((WIDTH, WIDTH), BF16),
            pltpu.VMEM((WIDTH, WIDTH), BF16),
            pltpu.VMEM((WIDTH, EMBED), BF16),
            pltpu.VMEM((ROWS, WIDTH), BF16),
            pltpu.VMEM((SEQ, 2, ROWS, HEAD), BF16),
            pltpu.VMEM((SEQ, 2, ROWS, HEAD), BF16),
            pltpu.VMEM((SEQ, ROWS, HEAD), BF16),
            pltpu.VMEM((SEQ, ROWS, HEAD), BF16),
            pltpu.VMEM((SEQ, ROWS, HEAD), BF16),
            pltpu.VMEM((SEQ, ROWS, HEAD), BF16),
            pltpu.VMEM((ROWS, WIDTH), BF16),
            pltpu.VMEM((POOL, ROWS, EMBED), BF16),
            pltpu.VMEM((POOL, EMBED, ROWS), BF16),
            pltpu.VMEM((POOL, 1, ROWS), jnp.int32),
            pltpu.VMEM((POOL, ROWS, ROWS), F32),
            pltpu.VMEM((POOL, ROWS, ROWS), F32),
            pltpu.VMEM((EMBED, ROWS), F32),
            pltpu.VMEM((8, ROWS, EMBED), BF16),
            pltpu.VMEM((8, ROWS, EMBED), BF16),
            pltpu.VMEM((8, ROWS, EMBED), F32),
            pltpu.VMEM((4, ROWS, EMBED), BF16),
            pltpu.VMEM((4, ROWS, EMBED), BF16),
            pltpu.VMEM((4, ROWS, EMBED), BF16),
            pltpu.VMEM((4, ROWS, EMBED), BF16),
            pltpu.VMEM((SEQ, 32, ROWS), BF16),
            pltpu.VMEM((SEQ, 32, ROWS), BF16),
            pltpu.VMEM((WIDTH // 2, EMBED), BF16),
            pltpu.VMEM((WIDTH // 2, EMBED), BF16),
            pltpu.VMEM((WIDTH // 2, EMBED), F32),
            pltpu.VMEM((SEQ, 64, EMBED), BF16),
            pltpu.VMEM((SEQ, 64, EMBED), BF16),
            pltpu.VMEM((GRID, 64, EMBED), BF16),
            pltpu.VMEM((16, 64, EMBED), BF16),
            dma((27,)),
            dma((2, SEQ)),
            dma((2, SEQ)),
            dma((2, SEQ)),
            dma((2, POOL)),
            dma((2, POOL)),
            dma((2, 8)),
            dma((2, 4)),
            dma((2, 4)),
            dma((2, SEQ)),
            dma((2,)),
            dma((2, SEQ)),
            dma((2, GRID)),
            dma((2, SEQ)),
            dma((2, SEQ)),
        ],
        compiler_params=pltpu.CompilerParams(
            collective_id=0, has_side_effects=True, vmem_limit_bytes=56 * 1024 * 1024
        ),
    )(
        tokens[0],
        w_in,
        w_out,
        w_proj,
        pos_embed[0],
        pos_ids,
        lengths,
        neg_embed[0],
        neg_ids,
    )
    return (loss, d_neg[None], d_proj)


def solution(mesh):
    placed = (
        P(("batch", "pool"), "seq", None),
        P(),
        P(),
        P(),
        P(("batch", "pool"), "seq", None),
        P(("batch", "pool"), "seq"),
        P(("batch", "pool")),
        P("batch", "pool", None),
        P("batch", "pool"),
    )
    return jax.shard_map(
        body,
        mesh=mesh,
        in_specs=placed,
        out_specs=(P(("batch", "pool"), "seq"), P("batch", "pool", "seq"), P()),
        check_vma=False,
    )
```

```python
import math

import jax
import jax.numpy as jnp
from jax import lax
from jax.experimental import pallas as pl
from jax.experimental.pallas import tpu as pltpu
from jax.sharding import PartitionSpec as P

HEADS = 8
HEAD = 128
ROWS = 256
WIDTH = 1024
EMBED = 256
SEQ = 8
POOL = 16
BATCH = 2
GRID = 16
ITEMS = 1048576
HIST = 32
WARMTH = 0.02
NORM_EPSILON = 1e-05
UNIT_EPSILON = 1e-06
MESH = pl.DeviceIdType.MESH
F32 = jnp.float32
BF16 = jnp.bfloat16


def dot(a, b):
    return jnp.dot(a, b, preferred_element_type=F32)


def dot_nt(a, b):
    return lax.dot_general(a, b, (((1,), (1,)), ((), ())), preferred_element_type=F32)


def dot_tn(a, b):
    return lax.dot_general(a, b, (((0,), (0,)), ((), ())), preferred_element_type=F32)


def silu(v):
    half = 0.5 * v
    return half + half * jnp.tanh(half)


def layer_norm(inputs):
    center = inputs - jnp.mean(inputs, axis=-1, keepdims=True)
    spread = jnp.mean(center * center, axis=-1, keepdims=True)
    return center * lax.rsqrt(spread + NORM_EPSILON)


def inverse_chance(ids):
    z = 1.0 / (2.0 * ids + 3.0)
    z2 = z * z
    series = 1.0 / 17.0
    for odd in (15, 13, 11, 9, 7, 5, 3, 1):
        series = series * z2 + 1.0 / odd
    return math.log(ITEMS + 1.0) / (2.0 * z * series)


def far_first(i):
    return 4 + (1 - 2 * (i % 2)) * ((i + 1) // 2)


def remote(src, dst, send, recv, **device):
    return pltpu.make_async_remote_copy(
        src_ref=src, dst_ref=dst, send_sem=send, recv_sem=recv, device_id=device, device_id_type=MESH
    )


def kernel(
    tokens_hbm,
    w_in,
    w_out,
    w_proj,
    pos_hbm,
    pos_ids,
    lengths,
    neg_hbm,
    neg_ids,
    loss_ref,
    dneg_ref,
    dproj_ref,
    tokens,
    pos_embed,
    neg_embed,
    wkv,
    wq,
    wg,
    wo,
    wp,
    normed,
    kvs,
    kvr,
    qs,
    qr,
    osend,
    orecv,
    gate,
    negs,
    negs_t,
    ids_all,
    cmask,
    kept,
    wt,
    pos_t,
    neg_unit,
    cs,
    cr,
    own,
    xs,
    xr,
    ys,
    yr,
    ybs,
    ybr,
    xbs,
    xbr,
    neg_t,
    zs,
    zr,
    term,
    pcs,
    pcr,
    pxs,
    pxr,
    pzr,
    fin,
    w_sem,
    kv_sem,
    q_sem,
    o_sem,
    neg_sem,
    id_sem,
    c_sem,
    x_sem,
    y_sem,
    yb_sem,
    xb_sem,
    z_sem,
    pc_sem,
    px_sem,
    pz_sem,
    f_sem,
    fc_sem,
):
    b = lax.axis_index("batch")
    s = lax.axis_index("seq")
    p = lax.axis_index("pool")
    core = p % 2
    xlo = (p // 2) % 2
    y = p // 4
    sibling = p + 1 - 2 * core
    across = p + 2 - 4 * xlo
    q_own = b * 8 + p // 2

    def load_kv(k):
        h = (s + k) % SEQ
        return [
            pltpu.make_async_copy(
                w_in.at[:, pl.ds(pl.multiple_of(3 * WIDTH + h * HEAD, HEAD), HEAD)],
                wkv.at[k, :, pl.ds(0, HEAD)],
                w_sem.at[k],
            ),
            pltpu.make_async_copy(
                w_in.at[:, pl.ds(pl.multiple_of(WIDTH + h * HEAD, HEAD), HEAD)],
                wkv.at[k, :, pl.ds(HEAD, HEAD)],
                w_sem.at[8 + k],
            ),
        ]

    def load_q(i, half):
        h = (s + far_first(2 * i + half)) % SEQ
        return pltpu.make_async_copy(
            w_in.at[:, pl.ds(pl.multiple_of(2 * WIDTH + h * HEAD, HEAD), HEAD)],
            wq.at[i, :, pl.ds(half * HEAD, HEAD)],
            w_sem.at[16 + 2 * i + half],
        )

    load_g = pltpu.make_async_copy(w_in.at[:, pl.ds(0, WIDTH)], wg, w_sem.at[24])
    load_o = pltpu.make_async_copy(w_out, wo, w_sem.at[25])
    load_p = pltpu.make_async_copy(w_proj, wp, w_sem.at[26])
    load_t = pltpu.make_async_copy(tokens_hbm, tokens, w_sem.at[27])
    load_n = pltpu.make_async_copy(neg_hbm, neg_embed, w_sem.at[28])
    load_pos = pltpu.make_async_copy(pos_hbm, pos_embed, w_sem.at[29])
    load_t.start()
    for i in range(8):
        for c in load_kv(far_first(i)):
            c.start()
    for i in range(4):
        load_q(i, 0).start()
        load_q(i, 1).start()
    load_n.start()
    load_pos.start()
    load_g.start()
    load_o.start()
    load_p.start()

    barrier = pltpu.get_barrier_semaphore()

    @pl.loop(1, SEQ)
    def _(k):
        pl.semaphore_signal(barrier, inc=1, device_id={"seq": (s + k) % SEQ}, device_id_type=MESH)

    @pl.loop(1, POOL)
    def _(k):
        pl.semaphore_signal(barrier, inc=1, device_id={"pool": (p + k) % POOL}, device_id_type=MESH)

    @pl.loop(0, POOL // 2)
    def _(k):
        pl.semaphore_signal(
            barrier, inc=1, device_id={"batch": 1 - b, "pool": 2 * k + core}, device_id_type=MESH
        )

    load_t.wait()

    @pl.loop(0, 4)
    def _(i):
        rows = pl.ds(pl.multiple_of(i * 64, 64), 64)
        normed[rows, :] = layer_norm(tokens[rows, :].astype(F32)).astype(BF16)

    length = lengths[0]
    row_pos = s * ROWS + lax.broadcasted_iota(jnp.int32, (ROWS, 1), 0)
    row_valid = row_pos < length

    def send_kv(k):
        return remote(
            kvs.at[k], kvr.at[s], kv_sem.at[0, k], kv_sem.at[1, k], seq=(s + k) % SEQ
        )

    def recv_kv(k):
        return remote(
            kvs.at[k], kvr.at[(s + SEQ - k) % SEQ], kv_sem.at[0, k], kv_sem.at[1, k], seq=(s + k) % SEQ
        )

    @pl.loop(0, SEQ)
    def _(i):
        k = far_first(i)
        for c in load_kv(k):
            c.wait()
        both = silu(dot(normed[...], wkv[k]))
        keys = both[:, :HEAD].astype(BF16)
        values = jnp.where(row_valid, both[:, HEAD:], 0.0).astype(BF16)

        kvs[k, 0] = keys
        kvs[k, 1] = values

    pl.semaphore_wait(barrier, (SEQ - 1) + (POOL - 1) + POOL // 2)

    @pl.loop(0, SEQ - 1)
    def _(i):
        send_kv(far_first(i)).start()

    kvr[s] = kvs[0]

    def send_q(k):
        return remote(qs.at[k], qr.at[s], q_sem.at[0, k], q_sem.at[1, k], seq=(s + k) % SEQ)

    def recv_q(k):
        return remote(
            qs.at[k], qr.at[(s + SEQ - k) % SEQ], q_sem.at[0, k], q_sem.at[1, k], seq=(s + k) % SEQ
        )

    @pl.loop(0, SEQ // 2)
    def _(i):
        load_q(i, 0).wait()
        load_q(i, 1).wait()
        both = silu(dot(normed[...], wq[i])).astype(BF16)
        k0 = far_first(2 * i)
        k1 = far_first(2 * i + 1)
        qs[k0] = both[:, :HEAD]
        send_q(k0).start()

        @pl.when(i < SEQ // 2 - 1)
        def _():
            qs[k1] = both[:, HEAD:]
            send_q(k1).start()

        @pl.when(i == SEQ // 2 - 1)
        def _():
            qr[s] = both[:, HEAD:]

    load_n.wait()
    neg = neg_embed[...].astype(F32)
    neg_norm = jnp.sqrt(jnp.sum(neg * neg, axis=-1, keepdims=True) + UNIT_EPSILON)
    neg_unit[...] = neg / neg_norm
    negs[p] = neg_unit[...].astype(BF16)
    ids_all[p] = neg_ids[...]

    def send_ids(k):
        return remote(ids_all.at[p], ids_all.at[p], id_sem.at[0, k], id_sem.at[1, k], pool=(p + k) % POOL)

    def recv_ids(k):
        src = (p + POOL - k) % POOL
        return remote(ids_all.at[src], ids_all.at[src], id_sem.at[0, k], id_sem.at[1, k], pool=src)

    def send_negs(k):
        return remote(negs.at[p], negs.at[p], neg_sem.at[0, k], neg_sem.at[1, k], pool=(p + k) % POOL)

    def recv_negs(k):
        src = (p + POOL - k) % POOL
        return remote(negs.at[src], negs.at[src], neg_sem.at[0, k], neg_sem.at[1, k], pool=src)

    @pl.loop(1, POOL)
    def _(k):
        send_ids(k).start()

    @pl.loop(1, POOL)
    def _(k):
        send_negs(k).start()

    load_g.wait()

    @pl.loop(0, 4)
    def _(i):
        cols = pl.ds(pl.multiple_of(i * 256, 256), 256)
        gate[:, cols] = silu(dot(normed[...], wg[:, cols])).astype(BF16)

    load_pos.wait()
    pos = jnp.transpose(pos_embed[...].astype(F32))
    pos_t[...] = pos / jnp.sqrt(jnp.sum(pos * pos, axis=0, keepdims=True) + UNIT_EPSILON)
    pos_row = pos_ids[...]

    @pl.loop(1, POOL)
    def _(k):
        recv_ids(k).wait_recv()

    ids = jnp.concatenate([ids_all[j] for j in range(POOL)], axis=0)
    factor = jnp.transpose(inverse_chance(ids.astype(F32)))
    ids_col = jnp.transpose(ids.astype(F32)).astype(jnp.int32)
    for j in range(POOL):
        cmask[j] = jnp.where(ids_col[:, j : j + 1] != pos_row, factor[:, j : j + 1], 0.0)

    def send_o(k):
        dst = (s + SEQ - k) % SEQ
        return remote(osend.at[k], orecv.at[s], o_sem.at[0, k], o_sem.at[1, k], seq=dst)

    def recv_o(k):
        src = (s + k) % SEQ
        return remote(osend.at[k], orecv.at[src], o_sem.at[0, k], o_sem.at[1, k], seq=src)

    @pl.loop(1, SEQ)
    def _(k):
        recv_kv(k).wait_recv()

    scale = 0.5 / math.sqrt(HEAD)

    @pl.loop(0, SEQ)
    def _(i):
        k = far_first((i + SEQ - 1) % SEQ)
        a = (s + SEQ - k) % SEQ

        @pl.when(i > 0)
        def _():
            recv_q(k).wait_recv()

        query = qr[a]

        def weights(u):
            half = scale * dot_nt(query, kvr[u, 0])
            return half + half * jnp.tanh(half)

        def group(g, total):
            return (
                total
                + dot(weights(2 * g).astype(BF16), kvr[2 * g, 1])
                + dot(weights(2 * g + 1).astype(BF16), kvr[2 * g + 1, 1])
            )

        total = lax.fori_loop(0, a // 2, group, jnp.zeros((ROWS, HEAD), F32))
        last = 2 * (a // 2)
        t_pos = a * ROWS + lax.broadcasted_iota(jnp.int32, (ROWS, ROWS), 0)
        u_pos = lax.broadcasted_iota(jnp.int32, (ROWS, ROWS), 1)
        for u in (last, last + 1):
            seen = jnp.where(u * ROWS + u_pos <= t_pos, weights(u), 0.0).astype(BF16)
            total = total + dot(seen, kvr[u, 1])

        @pl.when(i > 0)
        def _():
            osend[k] = total.astype(BF16)
            send_o(k).start()

        @pl.when(i == 0)
        def _():
            orecv[s] = total.astype(BF16)

    @pl.loop(0, POOL)
    def _(k):
        @pl.when(k > 0)
        def _():
            recv_negs(k).wait_recv()

        src = (p + POOL - k) % POOL
        negs_t[:, pl.ds(pl.multiple_of(src * ROWS, ROWS), ROWS)] = jnp.transpose(negs[src])

    load_o.wait()
    load_p.wait()

    @pl.loop(1, SEQ)
    def _(k):
        recv_o(k).wait_recv()

    attn = jnp.concatenate([orecv[h] for h in range(HEADS)], axis=1).astype(F32)
    gated = (layer_norm(attn) * gate[...].astype(F32)).astype(BF16)
    layer_out = (dot(gated, wo[...]) + tokens[...].astype(F32)).astype(BF16)
    out = dot(layer_out, wp[...])
    out_hat = (out * lax.rsqrt(jnp.sum(out * out, axis=-1, keepdims=True) + UNIT_EPSILON)).astype(BF16)
    out_t = jnp.transpose(out)
    norm_t = jnp.sqrt(jnp.sum(out_t * out_t, axis=0, keepdims=True) + UNIT_EPSILON)
    unit_t = out_t / norm_t
    hat_t = unit_t.astype(BF16)
    pos_dot = jnp.sum(hat_t.astype(F32) * pos_t[...], axis=0, keepdims=True) * (1.0 / WARMTH)
    pos_chance = inverse_chance(pos_row.astype(F32))
    pos_logit = pos_dot + jnp.log(pos_chance)
    pos_exp = jnp.exp(pos_logit)

    def scores(j, total):
        value = jnp.exp(dot(negs[j], hat_t) * (1.0 / WARMTH)) * cmask[j]
        kept[j] = value
        return total + jnp.sum(value, axis=0, keepdims=True)

    total = lax.fori_loop(0, POOL, scores, jnp.zeros((1, ROWS), F32)) + pos_exp
    valid = s * ROWS + lax.broadcasted_iota(jnp.int32, (1, ROWS), 1) < length
    loss_ref[...] = jnp.where(valid, jnp.log(total) - pos_logit, 0.0)
    share = jnp.where(valid, 1.0 / (total * HIST), 0.0)
    pos_weight = jnp.where(valid, pos_exp / total - 1.0, 0.0) * (1.0 / HIST)

    @pl.loop(0, POOL)
    def _(j):
        wt[pl.ds(pl.multiple_of(j * ROWS, ROWS), ROWS), :] = (kept[j] * share).astype(BF16)

    rows_t = dot(negs_t[...], wt[...])
    grad_t = (pos_weight * pos_t[...] + rows_t) * (1.0 / WARMTH)
    d_out = jnp.transpose(
        (grad_t - unit_t * jnp.sum(unit_t * grad_t, axis=0, keepdims=True)) / norm_t
    ).astype(BF16)
    term[...] = dot_tn(layer_out, d_out)

    half = WIDTH // 2
    mine = pl.ds(pl.multiple_of(core * half, half), half)
    theirs = pl.ds(pl.multiple_of((1 - core) * half, half), half)
    pcs[...] = term[theirs, :].astype(BF16)
    send_pc = remote(pcs, pcr, pc_sem.at[0], pc_sem.at[1], pool=sibling)
    send_pc.start()

    def place(n):
        y_at = (y + 1 + n // 2) % 4
        x_at = xlo + (1 - n % 2) * (1 - 2 * xlo)
        return y_at, x_at

    def send_c(m):
        return remote(cs.at[m], cr.at[m], c_sem.at[0, m], c_sem.at[1, m], pool=sibling)

    def portion(j):
        weight = wt[pl.ds(pl.multiple_of(j * ROWS, ROWS), ROWS), :]
        return dot(weight, out_hat) * (1.0 / WARMTH)

    @pl.loop(0, 8)
    def _(n):
        y_at, x_at = place(n)
        m = 2 * y_at + x_at
        cs[m] = portion(2 * m + 1 - core).astype(BF16)
        send_c(m).start()

    def plane(q):
        return {"batch": q // 8, "pool": 2 * (q % 8) + core}

    def send_px(k):
        q = (q_own + k) % GRID
        return remote(
            pxs.at[pl.ds(pl.multiple_of(q * 32, 32), 32), :],
            pxr.at[q_own],
            px_sem.at[0, k],
            px_sem.at[1, k],
            **plane(q),
        )

    def recv_px(k):
        q = (q_own + GRID - k) % GRID
        return remote(
            pxs.at[pl.ds(0, 32), :], pxr.at[q], px_sem.at[0, k], px_sem.at[1, k], **plane(q)
        )

    send_pc.wait_recv()
    pxs[...] = (term[mine, :] + pcr[...].astype(F32)).astype(BF16)

    @pl.loop(1, GRID)
    def _(k):
        send_px(k).start()

    pxr[q_own] = pxs[pl.ds(pl.multiple_of(q_own * 32, 32), 32), :]

    def send_x(i):
        return remote(xs.at[i], xr.at[i], x_sem.at[0, i], x_sem.at[1, i], pool=across)

    def send_yb(k):
        return remote(
            ybs.at[k], ybr.at[k], yb_sem.at[0, k], yb_sem.at[1, k], pool=((y + k) % 4) * 4 + p % 4
        )

    @pl.loop(0, 8)
    def _(n):
        y_at, x_at = place(n)
        m = 2 * y_at + x_at
        mixed = portion(2 * m + core)
        send_c(m).wait_recv()
        mixed = mixed + cr[m].astype(F32)
        own[m] = mixed

        @pl.when(n % 2 == 0)
        def _():
            xs[y_at] = mixed[:128].astype(BF16)
            send_x(y_at).start()

        @pl.when(n < 6)
        def _():
            ybs[1 + n // 2, x_at] = mixed[128:].astype(BF16)

        @pl.when((n < 6) & (n % 2 == 1))
        def _():
            send_yb(1 + n // 2).start()

    def send_pz(k):
        return remote(pzr.at[s], pzr.at[s], pz_sem.at[0, k], pz_sem.at[1, k], seq=(s + k) % SEQ)

    def recv_pz(k):
        src = (s + SEQ - k) % SEQ
        return remote(pzr.at[src], pzr.at[src], pz_sem.at[0, k], pz_sem.at[1, k], seq=src)

    @pl.loop(1, GRID)
    def _(k):
        recv_px(k).wait_recv()

    block = pxr[0].astype(F32)
    for q in range(1, GRID):
        block = block + pxr[q].astype(F32)
    pzr[s] = block.astype(BF16)

    @pl.loop(1, SEQ)
    def _(k):
        send_pz(k).start()

    def send_y(k):
        return remote(
            ys.at[k], yr.at[k], y_sem.at[0, k], y_sem.at[1, k], pool=((y + k) % 4) * 4 + p % 4
        )

    send_xb = remote(xbs, xbr, xb_sem.at[0], xb_sem.at[1], pool=across)

    @pl.loop(1, 4)
    def _(k):
        i = (y + k) % 4
        send_x(i).wait_recv()
        ys[k] = (own[2 * i + xlo, :128] + xr[i].astype(F32)).astype(BF16)
        send_y(k).start()

    lower_theirs = own[2 * y + 1 - xlo, 128:]
    lower = own[2 * y + xlo, 128:]
    for k in range(1, 4):
        send_yb(k).wait_recv()
        lower_theirs = lower_theirs + ybr[k, 1 - xlo].astype(F32)
        lower = lower + ybr[k, xlo].astype(F32)
    xbs[...] = lower_theirs.astype(BF16)
    send_xb.start()
    send_x(y).wait_recv()
    own[2 * y + xlo, :128] = own[2 * y + xlo, :128] + xr[y].astype(F32)
    own[2 * y + xlo, 128:] = lower

    @pl.loop(1, SEQ)
    def _(k):
        recv_pz(k).wait_recv()

    whole = pzr[0].astype(F32)
    for z in range(1, SEQ):
        whole = whole + pzr[z].astype(F32)
    fin[core * GRID + q_own] = whole.astype(BF16)

    def send_f(k):
        at = core * GRID + q_own
        return remote(fin.at[at], fin.at[at], f_sem.at[0, k], f_sem.at[1, k], **plane((q_own + k) % GRID))

    def recv_f(k):
        q = (q_own + GRID - k) % GRID
        at = core * GRID + q
        return remote(fin.at[at], fin.at[at], f_sem.at[0, k], f_sem.at[1, k], **plane(q))

    def send_fc(k):
        at = core * GRID + (q_own + GRID - k) % GRID
        return remote(fin.at[at], fin.at[at], fc_sem.at[0, k], fc_sem.at[1, k], pool=sibling)

    def recv_fc(k):
        at = (1 - core) * GRID + (q_own + GRID - k) % GRID
        return remote(fin.at[at], fin.at[at], fc_sem.at[0, k], fc_sem.at[1, k], pool=sibling)

    @pl.loop(1, GRID)
    def _(k):
        send_f(k).start()

    send_fc(0).start()

    def send_z(k):
        return remote(zs.at[k], zr.at[k], z_sem.at[0, k], z_sem.at[1, k], seq=(s + k) % SEQ)

    upper = own[2 * y + xlo, :128]
    for k in range(1, 4):
        send_y(k).wait_recv()
        upper = upper + yr[k].astype(F32)
    send_xb.wait_recv()
    lower = own[2 * y + xlo, 128:] + xbr[...].astype(F32)
    neg_sum = jnp.concatenate([upper, lower], axis=0)
    neg = neg_embed[...].astype(F32)
    neg_norm = jnp.sqrt(jnp.sum(neg * neg, axis=-1, keepdims=True) + UNIT_EPSILON)
    unit = neg_unit[...]
    neg_t[...] = jnp.transpose(
        (neg_sum - unit * jnp.sum(unit * neg_sum, axis=-1, keepdims=True)) / neg_norm
    )

    @pl.loop(1, SEQ)
    def _(k):
        rows = pl.ds(pl.multiple_of(((s + k) % SEQ) * 32, 32), 32)
        zs[k] = neg_t[rows, :].astype(BF16)
        send_z(k).start()

    @pl.loop(1, GRID)
    def _(k):
        recv_f(k).wait_recv()
        send_fc(k).start()

    part = neg_t[pl.ds(pl.multiple_of(s * 32, 32), 32), :]
    for k in range(1, SEQ):
        send_z(k).wait_recv()
        part = part + zr[k].astype(F32)
    dneg_ref[...] = part

    @pl.loop(0, GRID)
    def _(k):
        recv_fc(k).wait_recv()

    dproj_ref[...] = fin[...]

    @pl.loop(1, SEQ)
    def _(k):
        send_kv(k).wait_send()
        send_q(k).wait_send()
        send_o(k).wait_send()
        send_pz(k).wait_send()
        send_z(k).wait_send()

    @pl.loop(1, POOL)
    def _(k):
        send_ids(k).wait_send()
        send_negs(k).wait_send()
        send_px(k).wait_send()
        send_f(k).wait_send()

    @pl.loop(0, GRID)
    def _(k):
        send_fc(k).wait_send()

    @pl.loop(0, 8)
    def _(m):
        send_c(m).wait_send()

    @pl.loop(0, 4)
    def _(i):
        send_x(i).wait_send()

    @pl.loop(1, 4)
    def _(k):
        send_y(k).wait_send()
        send_yb(k).wait_send()

    send_xb.wait_send()
    send_pc.wait_send()


def finish(loss, dneg_t, dproj, loss_out, dneg_out, dproj_out):
    loss_out[...] = loss[...]
    dneg_out[...] = dneg_t[...]
    dproj_out[...] = dproj[...].astype(F32)


def body(tokens, w_in, w_out, w_proj, pos_embed, pos_ids, lengths, neg_embed, neg_ids):
    vmem = pl.BlockSpec(memory_space=pltpu.VMEM)
    hbm = pl.BlockSpec(memory_space=pl.ANY)
    smem = pl.BlockSpec(memory_space=pltpu.SMEM)
    dma = pltpu.SemaphoreType.DMA
    loss, dneg_t, dproj = pl.pallas_call(
        kernel,
        out_shape=(
            jax.ShapeDtypeStruct((1, ROWS), F32),
            jax.ShapeDtypeStruct((EMBED // SEQ, ROWS), F32),
            jax.ShapeDtypeStruct((2 * GRID, 32, EMBED), BF16),
        ),
        in_specs=[hbm, hbm, hbm, hbm, hbm, vmem, smem, hbm, vmem],
        out_specs=(vmem, vmem, vmem),
        scratch_shapes=[
            pltpu.VMEM((ROWS, WIDTH), BF16),
            pltpu.VMEM((ROWS, EMBED), BF16),
            pltpu.VMEM((ROWS, EMBED), BF16),
            pltpu.VMEM((8, WIDTH, 256), BF16),
            pltpu.VMEM((4, WIDTH, 256), BF16),
            pltpu.VMEM((WIDTH, WIDTH), BF16),
            pltpu.VMEM((WIDTH, WIDTH), BF16),
            pltpu.VMEM((WIDTH, EMBED), BF16),
            pltpu.VMEM((ROWS, WIDTH), BF16),
            pltpu.VMEM((SEQ, 2, ROWS, HEAD), BF16),
            pltpu.VMEM((SEQ, 2, ROWS, HEAD), BF16),
            pltpu.VMEM((SEQ, ROWS, HEAD), BF16),
            pltpu.VMEM((SEQ, ROWS, HEAD), BF16),
            pltpu.VMEM((SEQ, ROWS, HEAD), BF16),
            pltpu.VMEM((SEQ, ROWS, HEAD), BF16),
            pltpu.VMEM((ROWS, WIDTH), BF16),
            pltpu.VMEM((POOL, ROWS, EMBED), BF16),
            pltpu.VMEM((EMBED, POOL * ROWS), BF16),
            pltpu.VMEM((POOL, 1, ROWS), jnp.int32),
            pltpu.VMEM((POOL, ROWS, ROWS), F32),
            pltpu.VMEM((POOL, ROWS, ROWS), F32),
            pltpu.VMEM((POOL * ROWS, ROWS), BF16),
            pltpu.VMEM((EMBED, ROWS), F32),
            pltpu.VMEM((ROWS, EMBED), F32),
            pltpu.VMEM((8, ROWS, EMBED), BF16),
            pltpu.VMEM((8, ROWS, EMBED), BF16),
            pltpu.VMEM((8, ROWS, EMBED), F32),
            pltpu.VMEM((4, 128, EMBED), BF16),
            pltpu.VMEM((4, 128, EMBED), BF16),
            pltpu.VMEM((4, 128, EMBED), BF16),
            pltpu.VMEM((4, 128, EMBED), BF16),
            pltpu.VMEM((4, 2, 128, EMBED), BF16),
            pltpu.VMEM((4, 2, 128, EMBED), BF16),
            pltpu.VMEM((128, EMBED), BF16),
            pltpu.VMEM((128, EMBED), BF16),
            pltpu.VMEM((EMBED, ROWS), F32),
            pltpu.VMEM((SEQ, 32, ROWS), BF16),
            pltpu.VMEM((SEQ, 32, ROWS), BF16),
            pltpu.VMEM((WIDTH, EMBED), F32),
            pltpu.VMEM((WIDTH // 2, EMBED), BF16),
            pltpu.VMEM((WIDTH // 2, EMBED), BF16),
            pltpu.VMEM((WIDTH // 2, EMBED), BF16),
            pltpu.VMEM((GRID, 32, EMBED), BF16),
            pltpu.VMEM((SEQ, 32, EMBED), BF16),
            pltpu.VMEM((2 * GRID, 32, EMBED), BF16),
            dma((30,)),
            dma((2, SEQ)),
            dma((2, SEQ)),
            dma((2, SEQ)),
            dma((2, POOL)),
            dma((2, POOL)),
            dma((2, 8)),
            dma((2, 4)),
            dma((2, 4)),
            dma((2, 4)),
            dma((2,)),
            dma((2, SEQ)),
            dma((2,)),
            dma((2, GRID)),
            dma((2, SEQ)),
            dma((2, GRID)),
            dma((2, GRID)),
        ],
        compiler_params=pltpu.CompilerParams(
            collective_id=0, has_side_effects=True, vmem_limit_bytes=56 * 1024 * 1024
        ),
    )(
        tokens[0],
        w_in,
        w_out,
        w_proj,
        pos_embed[0],
        pos_ids,
        lengths,
        neg_embed[0],
        neg_ids,
    )
    loss, dneg_t, dproj = pl.pallas_call(
        finish,
        out_shape=(
            jax.ShapeDtypeStruct((1, ROWS), F32),
            jax.ShapeDtypeStruct((EMBED // SEQ, ROWS), F32),
            jax.ShapeDtypeStruct((WIDTH, EMBED), F32),
        ),
        in_specs=[vmem, vmem, vmem],
        out_specs=(vmem, vmem, vmem),
    )(loss, dneg_t, dproj.reshape(WIDTH, EMBED))
    return (loss, jnp.transpose(dneg_t)[None], dproj)


def solution(mesh):
    placed = (
        P(("batch", "pool"), "seq", None),
        P(),
        P(),
        P(),
        P(("batch", "pool"), "seq", None),
        P(("batch", "pool"), "seq"),
        P(("batch", "pool")),
        P("batch", "pool", None),
        P("batch", "pool"),
    )
    return jax.shard_map(
        body,
        mesh=mesh,
        in_specs=placed,
        out_specs=(P(("batch", "pool"), "seq"), P("batch", "pool", "seq"), P()),
        check_vma=False,
    )
```

```python
import math

import jax
import jax.numpy as jnp
from jax import lax
from jax.experimental import pallas as pl
from jax.experimental.pallas import tpu as pltpu
from jax.sharding import PartitionSpec as P

HEADS = 8
HEAD = 128
ROWS = 256
HALF = 128
WIDTH = 1024
EMBED = 256
SEQ = 8
POOL = 16
BATCH = 2
GRID = 16
ITEMS = 1048576
HIST = 32
WARMTH = 0.02
NORM_EPSILON = 1e-05
UNIT_EPSILON = 1e-06
MESH = pl.DeviceIdType.MESH
F32 = jnp.float32
BF16 = jnp.bfloat16


def dot(a, b):
    return jnp.dot(a, b, preferred_element_type=F32)


def dot_nt(a, b):
    return lax.dot_general(a, b, (((1,), (1,)), ((), ())), preferred_element_type=F32)


def dot_tn(a, b):
    return lax.dot_general(a, b, (((0,), (0,)), ((), ())), preferred_element_type=F32)


def silu(v):
    half = 0.5 * v
    return half + half * jnp.tanh(half)


def layer_norm(inputs):
    center = inputs - jnp.mean(inputs, axis=-1, keepdims=True)
    spread = jnp.mean(center * center, axis=-1, keepdims=True)
    return center * lax.rsqrt(spread + NORM_EPSILON)


def inverse_chance(ids):
    z = 1.0 / (2.0 * ids + 3.0)
    z2 = z * z
    series = 1.0 / 17.0
    for odd in (15, 13, 11, 9, 7, 5, 3, 1):
        series = series * z2 + 1.0 / odd
    return math.log(ITEMS + 1.0) / (2.0 * z * series)


STEPS = sorted(
    [(dx, dy) for dx in range(4) for dy in range(4) if dx or dy],
    key=lambda d: -(min(d[0], 4 - d[0]) + min(d[1], 4 - d[1])),
)


def far_first(i):
    return 4 + (1 - 2 * (i % 2)) * ((i + 1) // 2)


def remote(src, dst, send, recv, **device):
    return pltpu.make_async_remote_copy(
        src_ref=src, dst_ref=dst, send_sem=send, recv_sem=recv, device_id=device, device_id_type=MESH
    )


def kernel(
    tokens_hbm,
    w_in,
    w_out,
    w_proj,
    pos_hbm,
    pos_ids_hbm,
    lengths_hbm,
    neg_hbm,
    neg_ids_hbm,
    loss_ref,
    dneg_ref,
    dproj_ref,
    tokens,
    pos_embed,
    neg_embed,
    pos_ids,
    neg_ids,
    lengths,
    wkv,
    wq,
    wg,
    wo,
    wp,
    normed,
    kvs,
    kvr,
    qs,
    qr,
    osend,
    orecv,
    gate,
    negs,
    negs_t,
    ids_all,
    cmask,
    kept,
    wt,
    layer_out,
    out_hat,
    d_out,
    pos_t,
    neg_unit,
    cs,
    cr,
    own,
    xs,
    xr,
    ys,
    yr,
    ybs,
    ybr,
    xbs,
    xbr,
    neg_t,
    zs,
    zr,
    term,
    pcs,
    pcr,
    pxs,
    pxr,
    pzr,
    fin,
    loss,
    dneg,
    w_sem,
    kv_sem,
    q_sem,
    o_sem,
    neg_sem,
    id_sem,
    c_sem,
    x_sem,
    y_sem,
    yb_sem,
    xb_sem,
    z_sem,
    pc_sem,
    px_sem,
    pz_sem,
    f_sem,
    fc_sem,
    out_sem,
):
    b = lax.axis_index("batch")
    s = lax.axis_index("seq")
    p = lax.axis_index("pool")
    core = p % 2
    xlo = (p // 2) % 2
    y = p // 4
    sibling = p + 1 - 2 * core
    across = p + 2 - 4 * xlo
    q_own = b * 8 + p // 2

    load_ids = [
        pltpu.make_async_copy(pos_ids_hbm, pos_ids, w_sem.at[30]),
        pltpu.make_async_copy(neg_ids_hbm, neg_ids, w_sem.at[31]),
        pltpu.make_async_copy(lengths_hbm, lengths, w_sem.at[32]),
    ]
    def load_kv(k):
        h = (s + k) % SEQ
        return [
            pltpu.make_async_copy(
                w_in.at[:, pl.ds(pl.multiple_of(3 * WIDTH + h * HEAD, HEAD), HEAD)],
                wkv.at[k, :, pl.ds(0, HEAD)],
                w_sem.at[k],
            ),
            pltpu.make_async_copy(
                w_in.at[:, pl.ds(pl.multiple_of(WIDTH + h * HEAD, HEAD), HEAD)],
                wkv.at[k, :, pl.ds(HEAD, HEAD)],
                w_sem.at[8 + k],
            ),
        ]

    def load_q(i, half):
        h = (s + far_first(2 * i + half)) % SEQ
        return pltpu.make_async_copy(
            w_in.at[:, pl.ds(pl.multiple_of(2 * WIDTH + h * HEAD, HEAD), HEAD)],
            wq.at[i, :, pl.ds(half * HEAD, HEAD)],
            w_sem.at[16 + 2 * i + half],
        )

    load_g = pltpu.make_async_copy(w_in.at[:, pl.ds(0, WIDTH)], wg, w_sem.at[24])
    load_o = pltpu.make_async_copy(w_out, wo, w_sem.at[25])
    load_p = pltpu.make_async_copy(w_proj, wp, w_sem.at[26])
    load_t = pltpu.make_async_copy(tokens_hbm, tokens, w_sem.at[27])
    load_n = pltpu.make_async_copy(neg_hbm, neg_embed, w_sem.at[28])
    load_pos = pltpu.make_async_copy(pos_hbm, pos_embed, w_sem.at[29])
    barrier = pltpu.get_barrier_semaphore()

    @pl.loop(1, SEQ)
    def _(k):
        pl.semaphore_signal(barrier, inc=1, device_id={"seq": (s + k) % SEQ}, device_id_type=MESH)

    @pl.loop(1, POOL)
    def _(k):
        pl.semaphore_signal(barrier, inc=1, device_id={"pool": (p + k) % POOL}, device_id_type=MESH)

    @pl.loop(0, POOL // 2)
    def _(k):
        pl.semaphore_signal(
            barrier, inc=1, device_id={"batch": 1 - b, "pool": 2 * k + core}, device_id_type=MESH
        )

    load_t.start()
    for c in load_kv(4) + load_ids:
        c.start()
    for i in range(1, 8):
        for c in load_kv(far_first(i)):
            c.start()
    for i in range(4):
        load_q(i, 0).start()
        load_q(i, 1).start()

    load_t.wait()

    normed[...] = layer_norm(tokens[...].astype(F32)).astype(BF16)

    for c in load_ids:
        c.wait()
    length = lengths[0]
    row_pos = s * ROWS + lax.broadcasted_iota(jnp.int32, (ROWS, 1), 0)
    row_valid = row_pos < length

    def send_kv(k):
        return remote(
            kvs.at[k], kvr.at[s], kv_sem.at[0, k], kv_sem.at[1, k], seq=(s + k) % SEQ
        )

    def recv_kv(k):
        return remote(
            kvs.at[k], kvr.at[(s + SEQ - k) % SEQ], kv_sem.at[0, k], kv_sem.at[1, k], seq=(s + k) % SEQ
        )

    def make_kv(k):
        for c in load_kv(k):
            c.wait()
        both = silu(dot(normed[...], wkv[k]))
        kvs[k, 0] = both[:, :HEAD].astype(BF16)
        kvs[k, 1] = jnp.where(row_valid, both[:, HEAD:], 0.0).astype(BF16)

    make_kv(4)
    pl.semaphore_wait(barrier, (SEQ - 1) + (POOL - 1) + POOL // 2)
    send_kv(4).start()

    @pl.loop(1, SEQ)
    def _(i):
        k = far_first(i)
        make_kv(k)

        @pl.when(i < SEQ - 1)
        def _():
            send_kv(k).start()

    kvr[s] = kvs[0]
    load_n.start()
    load_pos.start()
    load_g.start()
    load_o.start()
    load_p.start()

    def send_q(k):
        return remote(qs.at[k], qr.at[s], q_sem.at[0, k], q_sem.at[1, k], seq=(s + k) % SEQ)

    def recv_q(k):
        return remote(
            qs.at[k], qr.at[(s + SEQ - k) % SEQ], q_sem.at[0, k], q_sem.at[1, k], seq=(s + k) % SEQ
        )

    @pl.loop(0, SEQ // 2)
    def _(i):
        load_q(i, 0).wait()
        load_q(i, 1).wait()
        both = silu(dot(normed[...], wq[i])).astype(BF16)
        k0 = far_first(2 * i)
        k1 = far_first(2 * i + 1)
        qs[k0] = both[:, :HEAD]
        send_q(k0).start()

        @pl.when(i < SEQ // 2 - 1)
        def _():
            qs[k1] = both[:, HEAD:]
            send_q(k1).start()

        @pl.when(i == SEQ // 2 - 1)
        def _():
            qr[s] = both[:, HEAD:]

    load_n.wait()
    neg = neg_embed[...].astype(F32)
    neg_norm = jnp.sqrt(jnp.sum(neg * neg, axis=-1, keepdims=True) + UNIT_EPSILON)
    neg_unit[...] = neg / neg_norm
    negs[p] = neg_unit[...].astype(BF16)
    ids_all[p] = neg_ids[...]

    def send_ids(k):
        return remote(ids_all.at[p], ids_all.at[p], id_sem.at[0, k], id_sem.at[1, k], pool=(p + k) % POOL)

    def recv_ids(k):
        src = (p + POOL - k) % POOL
        return remote(ids_all.at[src], ids_all.at[src], id_sem.at[0, k], id_sem.at[1, k], pool=src)

    def send_negs(k):
        return remote(negs.at[p], negs.at[p], neg_sem.at[0, k], neg_sem.at[1, k], pool=(p + k) % POOL)

    def recv_negs(k):
        src = (p + POOL - k) % POOL
        return remote(negs.at[src], negs.at[src], neg_sem.at[0, k], neg_sem.at[1, k], pool=src)

    @pl.loop(1, POOL)
    def _(k):
        send_ids(k).start()

    @pl.loop(1, POOL)
    def _(k):
        send_negs(k).start()

    load_g.wait()

    @pl.loop(0, 4)
    def _(i):
        cols = pl.ds(pl.multiple_of(i * 256, 256), 256)
        gate[:, cols] = silu(dot(normed[...], wg[:, cols])).astype(BF16)

    load_pos.wait()
    pos = jnp.transpose(pos_embed[...].astype(F32))
    pos_t[...] = pos / jnp.sqrt(jnp.sum(pos * pos, axis=0, keepdims=True) + UNIT_EPSILON)
    pos_row = pos_ids[...]

    @pl.loop(1, POOL)
    def _(k):
        recv_ids(k).wait_recv()

    ids = jnp.concatenate([ids_all[j] for j in range(POOL)], axis=0)
    factor = jnp.transpose(inverse_chance(ids.astype(F32)))
    ids_col = jnp.transpose(ids.astype(F32)).astype(jnp.int32)
    for j in range(POOL):
        cmask[j] = jnp.where(ids_col[:, j : j + 1] != pos_row, factor[:, j : j + 1], 0.0)

    def half_rows(h):
        return pl.ds(h * HALF, HALF)

    def send_o(k, h):
        return remote(
            osend.at[k, half_rows(h)],
            orecv.at[s, half_rows(h)],
            o_sem.at[h, 0, k],
            o_sem.at[h, 1, k],
            seq=(s + SEQ - k) % SEQ,
        )

    def recv_o(k, h):
        src = (s + k) % SEQ
        return remote(
            osend.at[k, half_rows(h)],
            orecv.at[src, half_rows(h)],
            o_sem.at[h, 0, k],
            o_sem.at[h, 1, k],
            seq=src,
        )

    @pl.loop(1, SEQ)
    def _(k):
        recv_kv(k).wait_recv()

    scale = 0.5 / math.sqrt(HEAD)

    @pl.loop(0, SEQ)
    def _(i):
        k = far_first((i + SEQ - 1) % SEQ)
        a = (s + SEQ - k) % SEQ

        @pl.when(i > 0)
        def _():
            recv_q(k).wait_recv()

        query = qr[a]

        def weights(u):
            half = scale * dot_nt(query, kvr[u, 0])
            return half + half * jnp.tanh(half)

        def group(g, total):
            for u in range(4):
                total = total + dot(weights(4 * g + u).astype(BF16), kvr[4 * g + u, 1])
            return total

        total = lax.fori_loop(0, a // 4, group, jnp.zeros((ROWS, HEAD), F32))
        t_pos = a * ROWS + lax.broadcasted_iota(jnp.int32, (ROWS, ROWS), 0)
        u_pos = lax.broadcasted_iota(jnp.int32, (ROWS, ROWS), 1)
        for last in range(4):
            u = 4 * (a // 4) + last
            seen = jnp.where(u * ROWS + u_pos <= t_pos, weights(u), 0.0).astype(BF16)
            total = total + dot(seen, kvr[u, 1])

        @pl.when(i > 0)
        def _():
            osend[k] = total.astype(BF16)
            send_o(k, 0).start()

        @pl.when(i == 0)
        def _():
            orecv[s] = total.astype(BF16)

    @pl.loop(1, SEQ)
    def _(i):
        send_o(far_first(i - 1), 1).start()

    @pl.loop(0, POOL)
    def _(k):
        @pl.when(k > 0)
        def _():
            recv_negs(k).wait_recv()

        src = (p + POOL - k) % POOL
        negs_t[:, pl.ds(pl.multiple_of(src * ROWS, ROWS), ROWS)] = jnp.transpose(negs[src])

    load_o.wait()
    load_p.wait()

    @pl.loop(0, 2)
    def _(h):
        start = pl.multiple_of(h * HALF, HALF)
        rows = pl.ds(start, HALF)

        @pl.loop(1, SEQ)
        def _(k):
            recv_o(k, h).wait_recv()

        attn = jnp.concatenate([orecv[j, rows] for j in range(HEADS)], axis=1).astype(F32)
        gated = (layer_norm(attn) * gate[rows, :].astype(F32)).astype(BF16)
        layer_half = (dot(gated, wo[...]) + tokens[rows, :].astype(F32)).astype(BF16)
        layer_out[rows, :] = layer_half
        out = dot(layer_half, wp[...])
        out_hat[rows, :] = (
            out * lax.rsqrt(jnp.sum(out * out, axis=-1, keepdims=True) + UNIT_EPSILON)
        ).astype(BF16)
        out_t = jnp.transpose(out)
        norm_t = jnp.sqrt(jnp.sum(out_t * out_t, axis=0, keepdims=True) + UNIT_EPSILON)
        unit_t = out_t / norm_t
        hat_t = unit_t.astype(BF16)
        pos_half = pos_t[:, rows]
        pos_dot = jnp.sum(hat_t.astype(F32) * pos_half, axis=0, keepdims=True) * (1.0 / WARMTH)
        pos_logit = pos_dot + jnp.log(inverse_chance(pos_ids[:, rows].astype(F32)))
        pos_exp = jnp.exp(pos_logit)

        def scores(j, sums):
            value = jnp.exp(dot(negs[j], hat_t) * (1.0 / WARMTH)) * cmask[j, :, rows]
            kept[j] = value
            return sums + jnp.sum(value, axis=0, keepdims=True)

        total = lax.fori_loop(0, POOL, scores, pos_exp, unroll=8)
        valid = s * ROWS + start + lax.broadcasted_iota(jnp.int32, (1, HALF), 1) < length
        loss[:, rows] = jnp.where(valid, jnp.log(total) - pos_logit, 0.0)
        share = jnp.where(valid, 1.0 / (total * HIST), 0.0)
        pos_weight = jnp.where(valid, pos_exp / total - 1.0, 0.0) * (1.0 / HIST)

        @pl.loop(0, POOL, unroll=4)
        def _(j):
            wt[pl.ds(pl.multiple_of(j * ROWS, ROWS), ROWS), rows] = (kept[j] * share).astype(BF16)

        rows_t = dot(negs_t[...], wt[:, rows])
        grad_t = (pos_weight * pos_half + rows_t) * (1.0 / WARMTH)
        d_out[rows, :] = jnp.transpose(
            (grad_t - unit_t * jnp.sum(unit_t * grad_t, axis=0, keepdims=True)) / norm_t
        ).astype(BF16)

    out_loss = pltpu.make_async_copy(loss, loss_ref, out_sem.at[3])
    out_loss.start()

    half = WIDTH // 2
    mine = pl.ds(pl.multiple_of(core * half, half), half)
    theirs = pl.ds(pl.multiple_of((1 - core) * half, half), half)
    pcs[...] = dot_tn(layer_out[:, theirs], d_out[...]).astype(BF16)
    send_pc = remote(pcs, pcr, pc_sem.at[0], pc_sem.at[1], pool=sibling)
    send_pc.start()
    term[...] = dot_tn(layer_out[:, mine], d_out[...])

    def place(n):
        y_at = (y + 1 + n // 2) % 4
        x_at = xlo + (1 - n % 2) * (1 - 2 * xlo)
        return y_at, x_at

    def send_c(m):
        return remote(cs.at[m], cr.at[m], c_sem.at[0, m], c_sem.at[1, m], pool=sibling)

    def portion(j):
        weight = wt[pl.ds(pl.multiple_of(j * ROWS, ROWS), ROWS), :]
        return dot(weight, out_hat[...]) * (1.0 / WARMTH)

    @pl.loop(0, 4, unroll=2)
    def _(n):
        y_at, x_at = place(n)
        m = 2 * y_at + x_at
        cs[m] = portion(2 * m + 1 - core).astype(BF16)
        send_c(m).start()

    x = 2 * b + xlo

    def plane(n, sign):
        dx, dy = STEPS[n]
        x_at = (x + (dx if sign > 0 else 4 - dx)) % 4
        y_at = (y + (dy if sign > 0 else 4 - dy)) % 4
        q = (x_at // 2) * 8 + y_at * 2 + x_at % 2
        return q, {"batch": x_at // 2, "pool": y_at * 4 + (x_at % 2) * 2 + core}

    def send_px(n):
        q, device = plane(n, 1)
        return remote(
            pxs.at[pl.ds(pl.multiple_of(q * 32, 32), 32), :],
            pxr.at[q_own],
            px_sem.at[0, n],
            px_sem.at[1, n],
            **device,
        )

    def recv_px(n):
        q, device = plane(n, -1)
        return remote(pxs.at[pl.ds(0, 32), :], pxr.at[q], px_sem.at[0, n], px_sem.at[1, n], **device)

    send_pc.wait_recv()
    pxs[...] = (term[...] + pcr[...].astype(F32)).astype(BF16)
    for n in range(GRID - 1):
        send_px(n).start()

    @pl.loop(4, 8, unroll=2)
    def _(n):
        y_at, x_at = place(n)
        m = 2 * y_at + x_at
        cs[m] = portion(2 * m + 1 - core).astype(BF16)
        send_c(m).start()

    pxr[q_own] = pxs[pl.ds(pl.multiple_of(q_own * 32, 32), 32), :]

    def send_x(i):
        return remote(xs.at[i], xr.at[i], x_sem.at[0, i], x_sem.at[1, i], pool=across)

    def send_yb(k):
        return remote(
            ybs.at[k], ybr.at[k], yb_sem.at[0, k], yb_sem.at[1, k], pool=((y + k) % 4) * 4 + p % 4
        )

    @pl.loop(0, 4)
    def _(n):
        y_at = (y + 1 + n) % 4
        m_far = 2 * y_at + 1 - xlo
        m_near = 2 * y_at + xlo
        far = portion(2 * m_far + core)
        near = portion(2 * m_near + core)
        send_c(m_far).wait_recv()
        far = far + cr[m_far].astype(F32)
        xs[y_at] = far[:HALF].astype(BF16)
        send_x(y_at).start()
        send_c(m_near).wait_recv()
        near = near + cr[m_near].astype(F32)
        own[m_near] = near

        @pl.when(n < 3)
        def _():
            ybs[1 + n, 1 - xlo] = far[HALF:].astype(BF16)
            ybs[1 + n, xlo] = near[HALF:].astype(BF16)
            send_yb(1 + n).start()

        @pl.when(n == 3)
        def _():
            own[m_far] = far

    def send_pz(k):
        return remote(pzr.at[s], pzr.at[s], pz_sem.at[0, k], pz_sem.at[1, k], seq=(s + k) % SEQ)

    def recv_pz(k):
        src = (s + SEQ - k) % SEQ
        return remote(pzr.at[src], pzr.at[src], pz_sem.at[0, k], pz_sem.at[1, k], seq=src)

    for n in range(GRID - 1):
        recv_px(n).wait_recv()

    block = pxr[0].astype(F32)
    for q in range(1, GRID):
        block = block + pxr[q].astype(F32)
    pzr[s] = block.astype(BF16)

    @pl.loop(0, SEQ - 1)
    def _(i):
        send_pz(far_first(i)).start()

    def send_y(k):
        return remote(
            ys.at[k], yr.at[k], y_sem.at[0, k], y_sem.at[1, k], pool=((y + k) % 4) * 4 + p % 4
        )

    send_xb = remote(xbs, xbr, xb_sem.at[0], xb_sem.at[1], pool=across)

    @pl.loop(1, 4)
    def _(k):
        i = (y + k) % 4
        send_x(i).wait_recv()
        ys[k] = (own[2 * i + xlo, :128] + xr[i].astype(F32)).astype(BF16)
        send_y(k).start()

    lower_theirs = own[2 * y + 1 - xlo, 128:]
    lower = own[2 * y + xlo, 128:]
    for k in range(1, 4):
        send_yb(k).wait_recv()
        lower_theirs = lower_theirs + ybr[k, 1 - xlo].astype(F32)
        lower = lower + ybr[k, xlo].astype(F32)
    xbs[...] = lower_theirs.astype(BF16)
    send_xb.start()
    send_x(y).wait_recv()
    own[2 * y + xlo, :128] = own[2 * y + xlo, :128] + xr[y].astype(F32)
    own[2 * y + xlo, 128:] = lower

    @pl.loop(1, SEQ)
    def _(k):
        recv_pz(k).wait_recv()

    whole = pzr[0].astype(F32)
    for z in range(1, SEQ):
        whole = whole + pzr[z].astype(F32)
    fin[core * GRID + q_own] = whole.astype(BF16)

    def send_f(n):
        at = core * GRID + q_own
        return remote(fin.at[at], fin.at[at], f_sem.at[0, n], f_sem.at[1, n], **plane(n, 1)[1])

    def recv_f(n):
        q, device = plane(n, -1)
        at = core * GRID + q
        return remote(fin.at[at], fin.at[at], f_sem.at[0, n], f_sem.at[1, n], **device)

    ours = fin.at[pl.ds(core * GRID, GRID)]
    others = fin.at[pl.ds((1 - core) * GRID, GRID)]
    send_fc = remote(ours, ours, fc_sem.at[0], fc_sem.at[1], pool=sibling)
    recv_fc = remote(others, others, fc_sem.at[0], fc_sem.at[1], pool=sibling)
    out_ours = pltpu.make_async_copy(ours, dproj_ref.at[pl.ds(core * GRID, GRID)], out_sem.at[0])
    out_others = pltpu.make_async_copy(
        others, dproj_ref.at[pl.ds((1 - core) * GRID, GRID)], out_sem.at[1]
    )

    for n in range(GRID - 1):
        send_f(n).start()

    def send_z(h, k):
        return remote(
            zs.at[h, k], zr.at[h, k], z_sem.at[h, 0, k], z_sem.at[h, 1, k], seq=(s + k) % SEQ
        )

    def project(h, neg_sum):
        rows = slice(h * HALF, (h + 1) * HALF)
        neg = neg_embed[rows, :].astype(F32)
        neg_norm = jnp.sqrt(jnp.sum(neg * neg, axis=-1, keepdims=True) + UNIT_EPSILON)
        unit = neg_unit[rows, :]
        neg_t[:, rows] = jnp.transpose(
            (neg_sum - unit * jnp.sum(unit * neg_sum, axis=-1, keepdims=True)) / neg_norm
        )

        @pl.loop(0, SEQ - 1)
        def _(i):
            k = far_first(i)
            cols = pl.ds(pl.multiple_of(((s + k) % SEQ) * 32, 32), 32)
            zs[h, k] = neg_t[cols, rows].astype(BF16)
            send_z(h, k).start()

    send_xb.wait_recv()
    project(1, own[2 * y + xlo, HALF:] + xbr[...].astype(F32))
    upper = own[2 * y + xlo, :HALF]
    for k in range(1, 4):
        send_y(k).wait_recv()
        upper = upper + yr[k].astype(F32)
    project(0, upper)

    for n in range(GRID - 1):
        recv_f(n).wait_recv()
    send_fc.start()
    out_ours.start()

    for h in (1, 0):
        rows = slice(h * HALF, (h + 1) * HALF)
        part = neg_t[pl.ds(pl.multiple_of(s * 32, 32), 32), rows]
        for k in range(1, SEQ):
            send_z(h, k).wait_recv()
            part = part + zr[h, k].astype(F32)
        dneg[:, rows] = part
    out_dneg = pltpu.make_async_copy(dneg, dneg_ref, out_sem.at[2])
    out_dneg.start()

    recv_fc.wait_recv()
    out_others.start()

    @pl.loop(1, SEQ)
    def _(k):
        send_kv(k).wait_send()
        send_q(k).wait_send()
        send_o(k, 0).wait_send()
        send_o(k, 1).wait_send()
        send_pz(k).wait_send()
        send_z(0, k).wait_send()
        send_z(1, k).wait_send()

    @pl.loop(1, POOL)
    def _(k):
        send_ids(k).wait_send()
        send_negs(k).wait_send()

    for n in range(GRID - 1):
        send_px(n).wait_send()
        send_f(n).wait_send()

    @pl.loop(0, 8)
    def _(m):
        send_c(m).wait_send()

    @pl.loop(0, 4)
    def _(i):
        send_x(i).wait_send()

    @pl.loop(1, 4)
    def _(k):
        send_y(k).wait_send()
        send_yb(k).wait_send()

    send_xb.wait_send()
    send_pc.wait_send()
    send_fc.wait_send()
    out_loss.wait()
    out_dneg.wait()
    out_ours.wait()
    out_others.wait()


def finish(loss, dneg_t, dproj, loss_out, dneg_out, dproj_out):
    loss_out[...] = loss[...]
    dneg_out[...] = dneg_t[...]
    dproj_out[...] = dproj[...].astype(F32)


def body(tokens, w_in, w_out, w_proj, pos_embed, pos_ids, lengths, neg_embed, neg_ids):
    vmem = pl.BlockSpec(memory_space=pltpu.VMEM)
    hbm = pl.BlockSpec(memory_space=pl.ANY)
    dma = pltpu.SemaphoreType.DMA
    loss, dneg_t, dproj = pl.pallas_call(
        kernel,
        out_shape=(
            jax.ShapeDtypeStruct((1, ROWS), F32),
            jax.ShapeDtypeStruct((EMBED // SEQ, ROWS), F32),
            jax.ShapeDtypeStruct((2 * GRID, 32, EMBED), BF16),
        ),
        in_specs=[hbm] * 9,
        out_specs=(hbm, hbm, hbm),
        scratch_shapes=[
            pltpu.VMEM((ROWS, WIDTH), BF16),
            pltpu.VMEM((ROWS, EMBED), BF16),
            pltpu.VMEM((ROWS, EMBED), BF16),
            pltpu.VMEM((1, ROWS), jnp.int32),
            pltpu.VMEM((1, ROWS), jnp.int32),
            pltpu.SMEM((1,), jnp.int32),
            pltpu.VMEM((8, WIDTH, 256), BF16),
            pltpu.VMEM((4, WIDTH, 256), BF16),
            pltpu.VMEM((WIDTH, WIDTH), BF16),
            pltpu.VMEM((WIDTH, WIDTH), BF16),
            pltpu.VMEM((WIDTH, EMBED), BF16),
            pltpu.VMEM((ROWS, WIDTH), BF16),
            pltpu.VMEM((SEQ, 2, ROWS, HEAD), BF16),
            pltpu.VMEM((SEQ, 2, ROWS, HEAD), BF16),
            pltpu.VMEM((SEQ, ROWS, HEAD), BF16),
            pltpu.VMEM((SEQ, ROWS, HEAD), BF16),
            pltpu.VMEM((SEQ, ROWS, HEAD), BF16),
            pltpu.VMEM((SEQ, ROWS, HEAD), BF16),
            pltpu.VMEM((ROWS, WIDTH), BF16),
            pltpu.VMEM((POOL, ROWS, EMBED), BF16),
            pltpu.VMEM((EMBED, POOL * ROWS), BF16),
            pltpu.VMEM((POOL, 1, ROWS), jnp.int32),
            pltpu.VMEM((POOL, ROWS, ROWS), F32),
            pltpu.VMEM((POOL, ROWS, HALF), F32),
            pltpu.VMEM((POOL * ROWS, ROWS), BF16),
            pltpu.VMEM((ROWS, WIDTH), BF16),
            pltpu.VMEM((ROWS, EMBED), BF16),
            pltpu.VMEM((ROWS, EMBED), BF16),
            pltpu.VMEM((EMBED, ROWS), F32),
            pltpu.VMEM((ROWS, EMBED), F32),
            pltpu.VMEM((8, ROWS, EMBED), BF16),
            pltpu.VMEM((8, ROWS, EMBED), BF16),
            pltpu.VMEM((8, ROWS, EMBED), F32),
            pltpu.VMEM((4, 128, EMBED), BF16),
            pltpu.VMEM((4, 128, EMBED), BF16),
            pltpu.VMEM((4, 128, EMBED), BF16),
            pltpu.VMEM((4, 128, EMBED), BF16),
            pltpu.VMEM((4, 2, 128, EMBED), BF16),
            pltpu.VMEM((4, 2, 128, EMBED), BF16),
            pltpu.VMEM((128, EMBED), BF16),
            pltpu.VMEM((128, EMBED), BF16),
            pltpu.VMEM((EMBED, ROWS), F32),
            pltpu.VMEM((2, SEQ, 32, HALF), BF16),
            pltpu.VMEM((2, SEQ, 32, HALF), BF16),
            pltpu.VMEM((WIDTH // 2, EMBED), F32),
            pltpu.VMEM((WIDTH // 2, EMBED), BF16),
            pltpu.VMEM((WIDTH // 2, EMBED), BF16),
            pltpu.VMEM((WIDTH // 2, EMBED), BF16),
            pltpu.VMEM((GRID, 32, EMBED), BF16),
            pltpu.VMEM((SEQ, 32, EMBED), BF16),
            pltpu.VMEM((2 * GRID, 32, EMBED), BF16),
            pltpu.VMEM((1, ROWS), F32),
            pltpu.VMEM((EMBED // SEQ, ROWS), F32),
            dma((33,)),
            dma((2, SEQ)),
            dma((2, SEQ)),
            dma((2, 2, SEQ)),
            dma((2, POOL)),
            dma((2, POOL)),
            dma((2, 8)),
            dma((2, 4)),
            dma((2, 4)),
            dma((2, 4)),
            dma((2,)),
            dma((2, 2, SEQ)),
            dma((2,)),
            dma((2, GRID)),
            dma((2, SEQ)),
            dma((2, GRID)),
            dma((2,)),
            dma((4,)),
        ],
        compiler_params=pltpu.CompilerParams(
            collective_id=0, has_side_effects=True, vmem_limit_bytes=56 * 1024 * 1024
        ),
    )(
        tokens[0],
        w_in,
        w_out,
        w_proj,
        pos_embed[0],
        pos_ids,
        lengths,
        neg_embed[0],
        neg_ids,
    )
    loss, dneg_t, dproj = pl.pallas_call(
        finish,
        out_shape=(
            jax.ShapeDtypeStruct((1, ROWS), F32),
            jax.ShapeDtypeStruct((EMBED // SEQ, ROWS), F32),
            jax.ShapeDtypeStruct((WIDTH, EMBED), F32),
        ),
        in_specs=[vmem, vmem, vmem],
        out_specs=(vmem, vmem, vmem),
    )(loss, dneg_t, dproj.reshape(WIDTH, EMBED))
    return (loss, jnp.transpose(dneg_t)[None], dproj)


def solution(mesh):
    placed = (
        P(("batch", "pool"), "seq", None),
        P(),
        P(),
        P(),
        P(("batch", "pool"), "seq", None),
        P(("batch", "pool"), "seq"),
        P(("batch", "pool")),
        P("batch", "pool", None),
        P("batch", "pool"),
    )
    return jax.shard_map(
        body,
        mesh=mesh,
        in_specs=placed,
        out_specs=(P(("batch", "pool"), "seq"), P("batch", "pool", "seq"), P()),
        check_vma=False,
    )
```

```python
import math

import jax
import jax.numpy as jnp
from jax import lax
from jax.experimental import pallas as pl
from jax.experimental.pallas import tpu as pltpu
from jax.sharding import PartitionSpec as P

HEADS = 8
HEAD = 128
ROWS = 256
HALF = 128
WIDTH = 1024
EMBED = 256
SEQ = 8
POOL = 16
BATCH = 2
GRID = 16
ITEMS = 1048576
HIST = 32
WARMTH = 0.02
NORM_EPSILON = 1e-05
UNIT_EPSILON = 1e-06
MESH = pl.DeviceIdType.MESH
F32 = jnp.float32
BF16 = jnp.bfloat16


def dot(a, b):
    return jnp.dot(a, b, preferred_element_type=F32)


def dot_nt(a, b):
    return lax.dot_general(a, b, (((1,), (1,)), ((), ())), preferred_element_type=F32)


def dot_tn(a, b):
    return lax.dot_general(a, b, (((0,), (0,)), ((), ())), preferred_element_type=F32)


def silu(v):
    half = 0.5 * v
    return half + half * jnp.tanh(half)


def layer_norm(inputs):
    center = inputs - jnp.mean(inputs, axis=-1, keepdims=True)
    spread = jnp.mean(center * center, axis=-1, keepdims=True)
    return center * lax.rsqrt(spread + NORM_EPSILON)


def inverse_chance(ids):
    z = 1.0 / (2.0 * ids + 3.0)
    z2 = z * z
    series = 1.0 / 17.0
    for odd in (15, 13, 11, 9, 7, 5, 3, 1):
        series = series * z2 + 1.0 / odd
    return math.log(ITEMS + 1.0) / (2.0 * z * series)


STEPS = sorted(
    [(dx, dy) for dx in range(4) for dy in range(4) if dx or dy],
    key=lambda d: -(min(d[0], 4 - d[0]) + min(d[1], 4 - d[1])),
)


def far_first(i):
    return 4 + (1 - 2 * (i % 2)) * ((i + 1) // 2)


def remote(src, dst, send, recv, **device):
    return pltpu.make_async_remote_copy(
        src_ref=src, dst_ref=dst, send_sem=send, recv_sem=recv, device_id=device, device_id_type=MESH
    )


def kernel(
    tokens_hbm,
    w_in,
    w_out,
    w_proj,
    pos_hbm,
    pos_ids_hbm,
    lengths_hbm,
    neg_hbm,
    neg_ids_hbm,
    loss_ref,
    dneg_ref,
    dproj_ref,
    tokens,
    pos_embed,
    neg_embed,
    pos_ids,
    neg_ids,
    lengths,
    wkv,
    wq,
    wg,
    wo,
    wp,
    normed,
    kvs,
    kvr,
    qs,
    qr,
    osend,
    orecv,
    gate,
    negs,
    negs_t,
    ids_all,
    cmask,
    kept,
    wt,
    layer_out,
    out_hat,
    d_out,
    pos_t,
    neg_unit,
    cs,
    cr,
    own,
    xs,
    xr,
    ys,
    yr,
    ybs,
    ybr,
    xbs,
    xbr,
    neg_t,
    zs,
    zr,
    term,
    pcs,
    pcr,
    pxs,
    pxr,
    pzr,
    fin,
    loss,
    dneg,
    w_sem,
    kv_sem,
    q_sem,
    o_sem,
    neg_sem,
    id_sem,
    c_sem,
    x_sem,
    y_sem,
    yb_sem,
    xb_sem,
    z_sem,
    pc_sem,
    px_sem,
    pz_sem,
    f_sem,
    fc_sem,
    out_sem,
):
    b = lax.axis_index("batch")
    s = lax.axis_index("seq")
    p = lax.axis_index("pool")
    core = p % 2
    xlo = (p // 2) % 2
    y = p // 4
    sibling = p + 1 - 2 * core
    across = p + 2 - 4 * xlo
    q_own = b * 8 + p // 2

    load_ids = [
        pltpu.make_async_copy(pos_ids_hbm, pos_ids, w_sem.at[30]),
        pltpu.make_async_copy(neg_ids_hbm, neg_ids, w_sem.at[31]),
        pltpu.make_async_copy(lengths_hbm, lengths, w_sem.at[32]),
    ]
    def load_kv(k):
        h = (s + k) % SEQ
        return [
            pltpu.make_async_copy(
                w_in.at[:, pl.ds(pl.multiple_of(3 * WIDTH + h * HEAD, HEAD), HEAD)],
                wkv.at[k, :, pl.ds(0, HEAD)],
                w_sem.at[k],
            ),
            pltpu.make_async_copy(
                w_in.at[:, pl.ds(pl.multiple_of(WIDTH + h * HEAD, HEAD), HEAD)],
                wkv.at[k, :, pl.ds(HEAD, HEAD)],
                w_sem.at[8 + k],
            ),
        ]

    def load_q(i, half):
        h = (s + far_first(2 * i + half)) % SEQ
        return pltpu.make_async_copy(
            w_in.at[:, pl.ds(pl.multiple_of(2 * WIDTH + h * HEAD, HEAD), HEAD)],
            wq.at[i, :, pl.ds(half * HEAD, HEAD)],
            w_sem.at[16 + 2 * i + half],
        )

    load_g = pltpu.make_async_copy(w_in.at[:, pl.ds(0, WIDTH)], wg, w_sem.at[24])
    load_o = pltpu.make_async_copy(w_out, wo, w_sem.at[25])
    load_p = pltpu.make_async_copy(w_proj, wp, w_sem.at[26])
    load_t = pltpu.make_async_copy(tokens_hbm, tokens, w_sem.at[27])
    load_n = pltpu.make_async_copy(neg_hbm, neg_embed, w_sem.at[28])
    load_pos = pltpu.make_async_copy(pos_hbm, pos_embed, w_sem.at[29])
    barrier = pltpu.get_barrier_semaphore()

    @pl.loop(1, SEQ)
    def _(k):
        pl.semaphore_signal(barrier, inc=1, device_id={"seq": (s + k) % SEQ}, device_id_type=MESH)

    @pl.loop(1, POOL)
    def _(k):
        pl.semaphore_signal(barrier, inc=1, device_id={"pool": (p + k) % POOL}, device_id_type=MESH)

    @pl.loop(0, POOL // 2)
    def _(k):
        pl.semaphore_signal(
            barrier, inc=1, device_id={"batch": 1 - b, "pool": 2 * k + core}, device_id_type=MESH
        )

    load_t.start()
    for c in load_kv(4) + load_ids:
        c.start()
    for i in range(1, 8):
        for c in load_kv(far_first(i)):
            c.start()
    for i in range(4):
        load_q(i, 0).start()
        load_q(i, 1).start()

    load_t.wait()

    normed[...] = layer_norm(tokens[...].astype(F32)).astype(BF16)

    for c in load_ids:
        c.wait()
    length = lengths[0]
    row_pos = s * ROWS + lax.broadcasted_iota(jnp.int32, (ROWS, 1), 0)
    row_valid = row_pos < length

    def send_kv(k):
        return remote(
            kvs.at[k], kvr.at[s], kv_sem.at[0, k], kv_sem.at[1, k], seq=(s + k) % SEQ
        )

    def recv_kv(k):
        return remote(
            kvs.at[k], kvr.at[(s + SEQ - k) % SEQ], kv_sem.at[0, k], kv_sem.at[1, k], seq=(s + k) % SEQ
        )

    def make_kv(k):
        for c in load_kv(k):
            c.wait()
        both = silu(dot(normed[...], wkv[k]))
        kvs[k, 0] = both[:, :HEAD].astype(BF16)
        kvs[k, 1] = jnp.where(row_valid, both[:, HEAD:], 0.0).astype(BF16)

    make_kv(4)
    pl.semaphore_wait(barrier, (SEQ - 1) + (POOL - 1) + POOL // 2)
    send_kv(4).start()

    @pl.loop(1, SEQ)
    def _(i):
        k = far_first(i)
        make_kv(k)

        @pl.when(i < SEQ - 1)
        def _():
            send_kv(k).start()

    kvr[s] = kvs[0]
    load_n.start()
    load_pos.start()
    load_g.start()
    load_o.start()
    load_p.start()

    def send_q(k):
        return remote(qs.at[k], qr.at[s], q_sem.at[0, k], q_sem.at[1, k], seq=(s + k) % SEQ)

    def recv_q(k):
        return remote(
            qs.at[k], qr.at[(s + SEQ - k) % SEQ], q_sem.at[0, k], q_sem.at[1, k], seq=(s + k) % SEQ
        )

    @pl.loop(0, SEQ // 2)
    def _(i):
        load_q(i, 0).wait()
        load_q(i, 1).wait()
        both = silu(dot(normed[...], wq[i])).astype(BF16)
        k0 = far_first(2 * i)
        k1 = far_first(2 * i + 1)
        qs[k0] = both[:, :HEAD]
        send_q(k0).start()

        @pl.when(i < SEQ // 2 - 1)
        def _():
            qs[k1] = both[:, HEAD:]
            send_q(k1).start()

        @pl.when(i == SEQ // 2 - 1)
        def _():
            qr[s] = both[:, HEAD:]

    load_n.wait()
    neg = neg_embed[...].astype(F32)
    neg_norm = jnp.sqrt(jnp.sum(neg * neg, axis=-1, keepdims=True) + UNIT_EPSILON)
    neg_unit[...] = neg / neg_norm
    negs[p] = neg_unit[...].astype(BF16)
    ids_all[p] = neg_ids[...]

    def send_ids(k):
        return remote(ids_all.at[p], ids_all.at[p], id_sem.at[0, k], id_sem.at[1, k], pool=(p + k) % POOL)

    def recv_ids(k):
        src = (p + POOL - k) % POOL
        return remote(ids_all.at[src], ids_all.at[src], id_sem.at[0, k], id_sem.at[1, k], pool=src)

    def send_negs(k):
        return remote(negs.at[p], negs.at[p], neg_sem.at[0, k], neg_sem.at[1, k], pool=(p + k) % POOL)

    def recv_negs(k):
        src = (p + POOL - k) % POOL
        return remote(negs.at[src], negs.at[src], neg_sem.at[0, k], neg_sem.at[1, k], pool=src)

    @pl.loop(1, POOL)
    def _(k):
        send_ids(k).start()

    @pl.loop(1, POOL)
    def _(k):
        send_negs(k).start()

    load_g.wait()

    @pl.loop(0, 4)
    def _(i):
        cols = pl.ds(pl.multiple_of(i * 256, 256), 256)
        gate[:, cols] = silu(dot(normed[...], wg[:, cols])).astype(BF16)

    load_pos.wait()
    pos = jnp.transpose(pos_embed[...].astype(F32))
    pos_t[...] = pos / jnp.sqrt(jnp.sum(pos * pos, axis=0, keepdims=True) + UNIT_EPSILON)
    pos_row = pos_ids[...]

    @pl.loop(1, POOL)
    def _(k):
        recv_ids(k).wait_recv()

    ids = jnp.concatenate([ids_all[j] for j in range(POOL)], axis=0)
    factor = jnp.transpose(inverse_chance(ids.astype(F32)))
    ids_col = jnp.transpose(ids.astype(F32)).astype(jnp.int32)
    for j in range(POOL):
        cmask[j] = jnp.where(ids_col[:, j : j + 1] != pos_row, factor[:, j : j + 1], 0.0)

    def half_rows(h):
        return pl.ds(h * HALF, HALF)

    def send_o(k, h):
        return remote(
            osend.at[k, half_rows(h)],
            orecv.at[s, half_rows(h)],
            o_sem.at[h, 0, k],
            o_sem.at[h, 1, k],
            seq=(s + SEQ - k) % SEQ,
        )

    def recv_o(k, h):
        src = (s + k) % SEQ
        return remote(
            osend.at[k, half_rows(h)],
            orecv.at[src, half_rows(h)],
            o_sem.at[h, 0, k],
            o_sem.at[h, 1, k],
            seq=src,
        )

    @pl.loop(1, SEQ)
    def _(k):
        recv_kv(k).wait_recv()

    scale = 0.5 / math.sqrt(HEAD)

    @pl.loop(0, SEQ)
    def _(i):
        k = far_first((i + SEQ - 1) % SEQ)
        a = (s + SEQ - k) % SEQ

        @pl.when(i > 0)
        def _():
            recv_q(k).wait_recv()

        query = qr[a]

        def weights(u):
            half = scale * dot_nt(query, kvr[u, 0])
            return half + half * jnp.tanh(half)

        def group(g, total):
            for u in range(4):
                total = total + dot(weights(4 * g + u).astype(BF16), kvr[4 * g + u, 1])
            return total

        total = lax.fori_loop(0, a // 4, group, jnp.zeros((ROWS, HEAD), F32))
        t_pos = a * ROWS + lax.broadcasted_iota(jnp.int32, (ROWS, ROWS), 0)
        u_pos = lax.broadcasted_iota(jnp.int32, (ROWS, ROWS), 1)
        for last in range(4):
            u = 4 * (a // 4) + last
            seen = jnp.where(u * ROWS + u_pos <= t_pos, weights(u), 0.0).astype(BF16)
            total = total + dot(seen, kvr[u, 1])

        @pl.when(i > 0)
        def _():
            osend[k] = total.astype(BF16)
            send_o(k, 0).start()

        @pl.when(i == 0)
        def _():
            orecv[s] = total.astype(BF16)

    @pl.loop(1, SEQ)
    def _(i):
        send_o(far_first(i - 1), 1).start()

    @pl.loop(1, SEQ)
    def _(k):
        send_kv(k).wait_send()
        send_q(k).wait_send()

    @pl.loop(1, POOL)
    def _(k):
        send_ids(k).wait_send()
        send_negs(k).wait_send()

    @pl.loop(0, POOL)
    def _(k):
        @pl.when(k > 0)
        def _():
            recv_negs(k).wait_recv()

        src = (p + POOL - k) % POOL
        negs_t[:, pl.ds(pl.multiple_of(src * ROWS, ROWS), ROWS)] = jnp.transpose(negs[src])

    load_o.wait()
    load_p.wait()

    @pl.loop(0, 2)
    def _(h):
        start = pl.multiple_of(h * HALF, HALF)
        rows = pl.ds(start, HALF)

        @pl.loop(1, SEQ)
        def _(k):
            recv_o(k, h).wait_recv()

        attn = jnp.concatenate([orecv[j, rows] for j in range(HEADS)], axis=1).astype(F32)
        gated = (layer_norm(attn) * gate[rows, :].astype(F32)).astype(BF16)
        layer_half = (dot(gated, wo[...]) + tokens[rows, :].astype(F32)).astype(BF16)
        layer_out[rows, :] = layer_half
        out = dot(layer_half, wp[...])
        out_hat[rows, :] = (
            out * lax.rsqrt(jnp.sum(out * out, axis=-1, keepdims=True) + UNIT_EPSILON)
        ).astype(BF16)
        out_t = jnp.transpose(out)
        norm_t = jnp.sqrt(jnp.sum(out_t * out_t, axis=0, keepdims=True) + UNIT_EPSILON)
        unit_t = out_t / norm_t
        hat_t = unit_t.astype(BF16)
        pos_half = pos_t[:, rows]
        pos_dot = jnp.sum(hat_t.astype(F32) * pos_half, axis=0, keepdims=True) * (1.0 / WARMTH)
        pos_logit = pos_dot + jnp.log(inverse_chance(pos_ids[:, rows].astype(F32)))
        pos_exp = jnp.exp(pos_logit)

        def scores(j, sums):
            value = jnp.exp(dot(negs[j], hat_t) * (1.0 / WARMTH)) * cmask[j, :, rows]
            kept[j] = value
            return sums + jnp.sum(value, axis=0, keepdims=True)

        total = lax.fori_loop(0, POOL, scores, pos_exp, unroll=8)
        valid = s * ROWS + start + lax.broadcasted_iota(jnp.int32, (1, HALF), 1) < length
        loss[:, rows] = jnp.where(valid, jnp.log(total) - pos_logit, 0.0)
        share = jnp.where(valid, 1.0 / (total * HIST), 0.0)
        pos_weight = jnp.where(valid, pos_exp / total - 1.0, 0.0) * (1.0 / HIST)

        @pl.loop(0, POOL, unroll=4)
        def _(j):
            wt[pl.ds(pl.multiple_of(j * ROWS, ROWS), ROWS), rows] = (kept[j] * share).astype(BF16)

        rows_t = dot(negs_t[...], wt[:, rows])
        grad_t = (pos_weight * pos_half + rows_t) * (1.0 / WARMTH)
        d_out[rows, :] = jnp.transpose(
            (grad_t - unit_t * jnp.sum(unit_t * grad_t, axis=0, keepdims=True)) / norm_t
        ).astype(BF16)

    out_loss = pltpu.make_async_copy(loss, loss_ref, out_sem.at[3])
    out_loss.start()

    half = WIDTH // 2
    mine = pl.ds(pl.multiple_of(core * half, half), half)
    theirs = pl.ds(pl.multiple_of((1 - core) * half, half), half)
    pcs[...] = dot_tn(layer_out[:, theirs], d_out[...]).astype(BF16)
    send_pc = remote(pcs, pcr, pc_sem.at[0], pc_sem.at[1], pool=sibling)
    send_pc.start()
    term[...] = dot_tn(layer_out[:, mine], d_out[...])

    def place(n):
        y_at = (y + 1 + n // 2) % 4
        x_at = xlo + (1 - n % 2) * (1 - 2 * xlo)
        return y_at, x_at

    def send_c(m):
        return remote(cs.at[m], cr.at[m], c_sem.at[0, m], c_sem.at[1, m], pool=sibling)

    def portion(j):
        weight = wt[pl.ds(pl.multiple_of(j * ROWS, ROWS), ROWS), :]
        return dot(weight, out_hat[...]) * (1.0 / WARMTH)

    @pl.loop(0, 4, unroll=2)
    def _(n):
        y_at, x_at = place(n)
        m = 2 * y_at + x_at
        cs[m] = portion(2 * m + 1 - core).astype(BF16)
        send_c(m).start()

    x = 2 * b + xlo

    def plane(n, sign):
        dx, dy = STEPS[n]
        x_at = (x + (dx if sign > 0 else 4 - dx)) % 4
        y_at = (y + (dy if sign > 0 else 4 - dy)) % 4
        q = (x_at // 2) * 8 + y_at * 2 + x_at % 2
        return q, {"batch": x_at // 2, "pool": y_at * 4 + (x_at % 2) * 2 + core}

    def send_px(n):
        q, device = plane(n, 1)
        return remote(
            pxs.at[pl.ds(pl.multiple_of(q * 32, 32), 32), :],
            pxr.at[q_own],
            px_sem.at[0, n],
            px_sem.at[1, n],
            **device,
        )

    def recv_px(n):
        q, device = plane(n, -1)
        return remote(pxs.at[pl.ds(0, 32), :], pxr.at[q], px_sem.at[0, n], px_sem.at[1, n], **device)

    send_pc.wait_recv()
    pxs[...] = (term[...] + pcr[...].astype(F32)).astype(BF16)
    for n in range(GRID - 1):
        send_px(n).start()

    @pl.loop(4, 8, unroll=2)
    def _(n):
        y_at, x_at = place(n)
        m = 2 * y_at + x_at
        cs[m] = portion(2 * m + 1 - core).astype(BF16)
        send_c(m).start()

    pxr[q_own] = pxs[pl.ds(pl.multiple_of(q_own * 32, 32), 32), :]

    def send_x(i):
        return remote(xs.at[i], xr.at[i], x_sem.at[0, i], x_sem.at[1, i], pool=across)

    def send_yb(k):
        return remote(
            ybs.at[k], ybr.at[k], yb_sem.at[0, k], yb_sem.at[1, k], pool=((y + k) % 4) * 4 + p % 4
        )

    @pl.loop(0, 4)
    def _(n):
        y_at = (y + 1 + n) % 4
        m_far = 2 * y_at + 1 - xlo
        m_near = 2 * y_at + xlo
        far = portion(2 * m_far + core)
        near = portion(2 * m_near + core)
        send_c(m_far).wait_recv()
        far = far + cr[m_far].astype(F32)
        xs[y_at] = far[:HALF].astype(BF16)
        send_x(y_at).start()
        send_c(m_near).wait_recv()
        near = near + cr[m_near].astype(F32)
        own[m_near] = near

        @pl.when(n < 3)
        def _():
            ybs[1 + n, 1 - xlo] = far[HALF:].astype(BF16)
            ybs[1 + n, xlo] = near[HALF:].astype(BF16)
            send_yb(1 + n).start()

        @pl.when(n == 3)
        def _():
            own[m_far] = far

    def send_pz(k):
        return remote(pzr.at[s], pzr.at[s], pz_sem.at[0, k], pz_sem.at[1, k], seq=(s + k) % SEQ)

    def recv_pz(k):
        src = (s + SEQ - k) % SEQ
        return remote(pzr.at[src], pzr.at[src], pz_sem.at[0, k], pz_sem.at[1, k], seq=src)

    for n in range(GRID - 1):
        recv_px(n).wait_recv()

    block = pxr[0].astype(F32)
    for q in range(1, GRID):
        block = block + pxr[q].astype(F32)
    pzr[s] = block.astype(BF16)

    @pl.loop(0, SEQ - 1)
    def _(i):
        send_pz(far_first(i)).start()

    @pl.loop(1, SEQ)
    def _(k):
        send_o(k, 0).wait_send()
        send_o(k, 1).wait_send()

    @pl.loop(0, 8)
    def _(m):
        send_c(m).wait_send()

    send_pc.wait_send()
    for n in range(GRID - 1):
        send_px(n).wait_send()

    def send_y(k):
        return remote(
            ys.at[k], yr.at[k], y_sem.at[0, k], y_sem.at[1, k], pool=((y + k) % 4) * 4 + p % 4
        )

    send_xb = remote(xbs, xbr, xb_sem.at[0], xb_sem.at[1], pool=across)

    @pl.loop(1, 4)
    def _(k):
        i = (y + k) % 4
        send_x(i).wait_recv()
        ys[k] = (own[2 * i + xlo, :128] + xr[i].astype(F32)).astype(BF16)
        send_y(k).start()

    lower_theirs = own[2 * y + 1 - xlo, 128:]
    lower = own[2 * y + xlo, 128:]
    for k in range(1, 4):
        send_yb(k).wait_recv()
        lower_theirs = lower_theirs + ybr[k, 1 - xlo].astype(F32)
        lower = lower + ybr[k, xlo].astype(F32)
    xbs[...] = lower_theirs.astype(BF16)
    send_xb.start()
    send_x(y).wait_recv()
    own[2 * y + xlo, :128] = own[2 * y + xlo, :128] + xr[y].astype(F32)
    own[2 * y + xlo, 128:] = lower

    @pl.loop(0, 4)
    def _(i):
        send_x(i).wait_send()

    @pl.loop(1, 4)
    def _(k):
        send_yb(k).wait_send()

    @pl.loop(1, SEQ)
    def _(k):
        recv_pz(k).wait_recv()

    whole = pzr[0].astype(F32)
    for z in range(1, SEQ):
        whole = whole + pzr[z].astype(F32)
    fin[core * GRID + q_own] = whole.astype(BF16)

    def send_f(n):
        at = core * GRID + q_own
        return remote(fin.at[at], fin.at[at], f_sem.at[0, n], f_sem.at[1, n], **plane(n, 1)[1])

    def recv_f(n):
        q, device = plane(n, -1)
        at = core * GRID + q
        return remote(fin.at[at], fin.at[at], f_sem.at[0, n], f_sem.at[1, n], **device)

    ours = fin.at[pl.ds(core * GRID, GRID)]
    others = fin.at[pl.ds((1 - core) * GRID, GRID)]
    send_fc = remote(ours, ours, fc_sem.at[0], fc_sem.at[1], pool=sibling)
    recv_fc = remote(others, others, fc_sem.at[0], fc_sem.at[1], pool=sibling)
    out_ours = pltpu.make_async_copy(ours, dproj_ref.at[pl.ds(core * GRID, GRID)], out_sem.at[0])
    out_others = pltpu.make_async_copy(
        others, dproj_ref.at[pl.ds((1 - core) * GRID, GRID)], out_sem.at[1]
    )

    for n in range(GRID - 1):
        send_f(n).start()

    def send_z(h, k):
        return remote(
            zs.at[h, k], zr.at[h, k], z_sem.at[h, 0, k], z_sem.at[h, 1, k], seq=(s + k) % SEQ
        )

    def project(h, neg_sum):
        rows = slice(h * HALF, (h + 1) * HALF)
        neg = neg_embed[rows, :].astype(F32)
        neg_norm = jnp.sqrt(jnp.sum(neg * neg, axis=-1, keepdims=True) + UNIT_EPSILON)
        unit = neg_unit[rows, :]
        neg_t[:, rows] = jnp.transpose(
            (neg_sum - unit * jnp.sum(unit * neg_sum, axis=-1, keepdims=True)) / neg_norm
        )

        @pl.loop(0, SEQ - 1)
        def _(i):
            k = far_first(i)
            cols = pl.ds(pl.multiple_of(((s + k) % SEQ) * 32, 32), 32)
            zs[h, k] = neg_t[cols, rows].astype(BF16)
            send_z(h, k).start()

    send_xb.wait_recv()
    project(1, own[2 * y + xlo, HALF:] + xbr[...].astype(F32))
    upper = own[2 * y + xlo, :HALF]
    for k in range(1, 4):
        send_y(k).wait_recv()
        upper = upper + yr[k].astype(F32)
    project(0, upper)

    @pl.loop(1, SEQ)
    def _(k):
        send_pz(k).wait_send()

    @pl.loop(1, 4)
    def _(k):
        send_y(k).wait_send()

    send_xb.wait_send()

    for n in range(GRID - 1):
        recv_f(n).wait_recv()
    send_fc.start()
    out_ours.start()
    for n in range(GRID - 1):
        send_f(n).wait_send()

    for h in (1, 0):
        rows = slice(h * HALF, (h + 1) * HALF)
        part = neg_t[pl.ds(pl.multiple_of(s * 32, 32), 32), rows]
        for k in range(1, SEQ):
            send_z(h, k).wait_recv()
            part = part + zr[h, k].astype(F32)
        dneg[:, rows] = part
    out_dneg = pltpu.make_async_copy(dneg, dneg_ref, out_sem.at[2])
    out_dneg.start()

    recv_fc.wait_recv()
    out_others.start()

    @pl.loop(1, SEQ)
    def _(k):
        send_z(0, k).wait_send()
        send_z(1, k).wait_send()

    send_fc.wait_send()
    out_loss.wait()
    out_dneg.wait()
    out_ours.wait()
    out_others.wait()


def finish(loss, dneg_t, dproj, loss_out, dneg_out, dproj_out):
    loss_out[...] = loss[...]
    dneg_out[...] = dneg_t[...]
    dproj_out[...] = dproj[...].astype(F32)


def body(tokens, w_in, w_out, w_proj, pos_embed, pos_ids, lengths, neg_embed, neg_ids):
    vmem = pl.BlockSpec(memory_space=pltpu.VMEM)
    hbm = pl.BlockSpec(memory_space=pl.ANY)
    dma = pltpu.SemaphoreType.DMA
    loss, dneg_t, dproj = pl.pallas_call(
        kernel,
        out_shape=(
            jax.ShapeDtypeStruct((1, ROWS), F32),
            jax.ShapeDtypeStruct((EMBED // SEQ, ROWS), F32),
            jax.ShapeDtypeStruct((2 * GRID, 32, EMBED), BF16),
        ),
        in_specs=[hbm] * 9,
        out_specs=(hbm, hbm, hbm),
        scratch_shapes=[
            pltpu.VMEM((ROWS, WIDTH), BF16),
            pltpu.VMEM((ROWS, EMBED), BF16),
            pltpu.VMEM((ROWS, EMBED), BF16),
            pltpu.VMEM((1, ROWS), jnp.int32),
            pltpu.VMEM((1, ROWS), jnp.int32),
            pltpu.SMEM((1,), jnp.int32),
            pltpu.VMEM((8, WIDTH, 256), BF16),
            pltpu.VMEM((4, WIDTH, 256), BF16),
            pltpu.VMEM((WIDTH, WIDTH), BF16),
            pltpu.VMEM((WIDTH, WIDTH), BF16),
            pltpu.VMEM((WIDTH, EMBED), BF16),
            pltpu.VMEM((ROWS, WIDTH), BF16),
            pltpu.VMEM((SEQ, 2, ROWS, HEAD), BF16),
            pltpu.VMEM((SEQ, 2, ROWS, HEAD), BF16),
            pltpu.VMEM((SEQ, ROWS, HEAD), BF16),
            pltpu.VMEM((SEQ, ROWS, HEAD), BF16),
            pltpu.VMEM((SEQ, ROWS, HEAD), BF16),
            pltpu.VMEM((SEQ, ROWS, HEAD), BF16),
            pltpu.VMEM((ROWS, WIDTH), BF16),
            pltpu.VMEM((POOL, ROWS, EMBED), BF16),
            pltpu.VMEM((EMBED, POOL * ROWS), BF16),
            pltpu.VMEM((POOL, 1, ROWS), jnp.int32),
            pltpu.VMEM((POOL, ROWS, ROWS), F32),
            pltpu.VMEM((POOL, ROWS, HALF), F32),
            pltpu.VMEM((POOL * ROWS, ROWS), BF16),
            pltpu.VMEM((ROWS, WIDTH), BF16),
            pltpu.VMEM((ROWS, EMBED), BF16),
            pltpu.VMEM((ROWS, EMBED), BF16),
            pltpu.VMEM((EMBED, ROWS), F32),
            pltpu.VMEM((ROWS, EMBED), F32),
            pltpu.VMEM((8, ROWS, EMBED), BF16),
            pltpu.VMEM((8, ROWS, EMBED), BF16),
            pltpu.VMEM((8, ROWS, EMBED), F32),
            pltpu.VMEM((4, 128, EMBED), BF16),
            pltpu.VMEM((4, 128, EMBED), BF16),
            pltpu.VMEM((4, 128, EMBED), BF16),
            pltpu.VMEM((4, 128, EMBED), BF16),
            pltpu.VMEM((4, 2, 128, EMBED), BF16),
            pltpu.VMEM((4, 2, 128, EMBED), BF16),
            pltpu.VMEM((128, EMBED), BF16),
            pltpu.VMEM((128, EMBED), BF16),
            pltpu.VMEM((EMBED, ROWS), F32),
            pltpu.VMEM((2, SEQ, 32, HALF), BF16),
            pltpu.VMEM((2, SEQ, 32, HALF), BF16),
            pltpu.VMEM((WIDTH // 2, EMBED), F32),
            pltpu.VMEM((WIDTH // 2, EMBED), BF16),
            pltpu.VMEM((WIDTH // 2, EMBED), BF16),
            pltpu.VMEM((WIDTH // 2, EMBED), BF16),
            pltpu.VMEM((GRID, 32, EMBED), BF16),
            pltpu.VMEM((SEQ, 32, EMBED), BF16),
            pltpu.VMEM((2 * GRID, 32, EMBED), BF16),
            pltpu.VMEM((1, ROWS), F32),
            pltpu.VMEM((EMBED // SEQ, ROWS), F32),
            dma((33,)),
            dma((2, SEQ)),
            dma((2, SEQ)),
            dma((2, 2, SEQ)),
            dma((2, POOL)),
            dma((2, POOL)),
            dma((2, 8)),
            dma((2, 4)),
            dma((2, 4)),
            dma((2, 4)),
            dma((2,)),
            dma((2, 2, SEQ)),
            dma((2,)),
            dma((2, GRID)),
            dma((2, SEQ)),
            dma((2, GRID)),
            dma((2,)),
            dma((4,)),
        ],
        compiler_params=pltpu.CompilerParams(
            collective_id=0, has_side_effects=True, vmem_limit_bytes=56 * 1024 * 1024
        ),
    )(
        tokens[0],
        w_in,
        w_out,
        w_proj,
        pos_embed[0],
        pos_ids,
        lengths,
        neg_embed[0],
        neg_ids,
    )
    loss, dneg_t, dproj = pl.pallas_call(
        finish,
        out_shape=(
            jax.ShapeDtypeStruct((1, ROWS), F32),
            jax.ShapeDtypeStruct((EMBED // SEQ, ROWS), F32),
            jax.ShapeDtypeStruct((WIDTH, EMBED), F32),
        ),
        in_specs=[vmem, vmem, vmem],
        out_specs=(vmem, vmem, vmem),
    )(loss, dneg_t, dproj.reshape(WIDTH, EMBED))
    return (loss, jnp.transpose(dneg_t)[None], dproj)


def solution(mesh):
    placed = (
        P(("batch", "pool"), "seq", None),
        P(),
        P(),
        P(),
        P(("batch", "pool"), "seq", None),
        P(("batch", "pool"), "seq"),
        P(("batch", "pool")),
        P("batch", "pool", None),
        P("batch", "pool"),
    )
    return jax.shard_map(
        body,
        mesh=mesh,
        in_specs=placed,
        out_specs=(P(("batch", "pool"), "seq"), P("batch", "pool", "seq"), P()),
        check_vma=False,
    )
```

```python
import math

import jax
import jax.numpy as jnp
from jax import lax
from jax.experimental import pallas as pl
from jax.experimental.pallas import tpu as pltpu
from jax.sharding import PartitionSpec as P

HEADS = 8
HEAD = 128
ROWS = 256
HALF = 128
WIDTH = 1024
EMBED = 256
SEQ = 8
POOL = 16
BATCH = 2
GRID = 16
ITEMS = 1048576
HIST = 32
WARMTH = 0.02
NORM_EPSILON = 1e-05
UNIT_EPSILON = 1e-06
MESH = pl.DeviceIdType.MESH
F32 = jnp.float32
BF16 = jnp.bfloat16


def dot(a, b):
    return jnp.dot(a, b, preferred_element_type=F32)


def dot_nt(a, b):
    return lax.dot_general(a, b, (((1,), (1,)), ((), ())), preferred_element_type=F32)


def dot_tn(a, b):
    return lax.dot_general(a, b, (((0,), (0,)), ((), ())), preferred_element_type=F32)


def silu(v):
    half = 0.5 * v
    return half + half * jnp.tanh(half)


def layer_norm(inputs):
    center = inputs - jnp.mean(inputs, axis=-1, keepdims=True)
    spread = jnp.mean(center * center, axis=-1, keepdims=True)
    return center * lax.rsqrt(spread + NORM_EPSILON)


def inverse_chance(ids):
    z = 1.0 / (2.0 * ids + 3.0)
    z2 = z * z
    series = 1.0 / 17.0
    for odd in (15, 13, 11, 9, 7, 5, 3, 1):
        series = series * z2 + 1.0 / odd
    return math.log(ITEMS + 1.0) / (2.0 * z * series)


STEPS = sorted(
    [(dx, dy) for dx in range(4) for dy in range(4) if dx or dy],
    key=lambda d: -(min(d[0], 4 - d[0]) + min(d[1], 4 - d[1])),
)


def far_first(i):
    return 4 + (1 - 2 * (i % 2)) * ((i + 1) // 2)


def near_first(i):
    return far_first((14 - i) % 8)


def remote(src, dst, send, recv, **device):
    return pltpu.make_async_remote_copy(
        src_ref=src, dst_ref=dst, send_sem=send, recv_sem=recv, device_id=device, device_id_type=MESH
    )


def kernel(
    tokens_hbm,
    w_in,
    w_out,
    w_proj,
    pos_hbm,
    pos_ids_hbm,
    lengths_hbm,
    neg_hbm,
    neg_ids_hbm,
    loss_ref,
    dneg_ref,
    dproj_ref,
    tokens,
    pos_embed,
    neg_embed,
    pos_ids,
    neg_ids,
    lengths,
    wkv,
    wq,
    wg,
    wo,
    wp,
    normed,
    kvs,
    kvr,
    qs,
    qr,
    osend,
    orecv,
    gate,
    negs,
    negs_t,
    ids_all,
    cmask,
    kept,
    wt,
    layer_out,
    out_hat,
    d_out,
    pos_t,
    neg_unit,
    cs,
    cr,
    own,
    xs,
    xr,
    ys,
    yr,
    ybs,
    ybr,
    xbs,
    xbr,
    neg_t,
    zs,
    zr,
    term,
    pcs,
    pcr,
    pxs,
    pxr,
    pzr,
    fin,
    loss,
    dneg,
    w_sem,
    kv_sem,
    q_sem,
    o_sem,
    neg_sem,
    id_sem,
    c_sem,
    x_sem,
    y_sem,
    yb_sem,
    xb_sem,
    z_sem,
    pc_sem,
    px_sem,
    pz_sem,
    f_sem,
    fc_sem,
    out_sem,
):
    b = lax.axis_index("batch")
    s = lax.axis_index("seq")
    p = lax.axis_index("pool")
    core = p % 2
    xlo = (p // 2) % 2
    y = p // 4
    sibling = p + 1 - 2 * core
    across = p + 2 - 4 * xlo
    q_own = b * 8 + p // 2

    load_ids = [
        pltpu.make_async_copy(pos_ids_hbm, pos_ids, w_sem.at[30]),
        pltpu.make_async_copy(neg_ids_hbm, neg_ids, w_sem.at[31]),
        pltpu.make_async_copy(lengths_hbm, lengths, w_sem.at[32]),
    ]
    def load_kv(k):
        h = (s + k) % SEQ
        return [
            pltpu.make_async_copy(
                w_in.at[:, pl.ds(pl.multiple_of(3 * WIDTH + h * HEAD, HEAD), HEAD)],
                wkv.at[k, :, pl.ds(0, HEAD)],
                w_sem.at[k],
            ),
            pltpu.make_async_copy(
                w_in.at[:, pl.ds(pl.multiple_of(WIDTH + h * HEAD, HEAD), HEAD)],
                wkv.at[k, :, pl.ds(HEAD, HEAD)],
                w_sem.at[8 + k],
            ),
        ]

    def load_q(i, half):
        h = (s + far_first(2 * i + half)) % SEQ
        return pltpu.make_async_copy(
            w_in.at[:, pl.ds(pl.multiple_of(2 * WIDTH + h * HEAD, HEAD), HEAD)],
            wq.at[i, :, pl.ds(half * HEAD, HEAD)],
            w_sem.at[16 + 2 * i + half],
        )

    load_g = pltpu.make_async_copy(w_in.at[:, pl.ds(0, WIDTH)], wg, w_sem.at[24])
    load_o = pltpu.make_async_copy(w_out, wo, w_sem.at[25])
    load_p = pltpu.make_async_copy(w_proj, wp, w_sem.at[26])
    load_t = pltpu.make_async_copy(tokens_hbm, tokens, w_sem.at[27])
    load_n = pltpu.make_async_copy(neg_hbm, neg_embed, w_sem.at[28])
    load_pos = pltpu.make_async_copy(pos_hbm, pos_embed, w_sem.at[29])
    barrier = pltpu.get_barrier_semaphore()

    @pl.loop(1, SEQ)
    def _(k):
        pl.semaphore_signal(barrier, inc=1, device_id={"seq": (s + k) % SEQ}, device_id_type=MESH)

    @pl.loop(1, POOL)
    def _(k):
        pl.semaphore_signal(barrier, inc=1, device_id={"pool": (p + k) % POOL}, device_id_type=MESH)

    @pl.loop(0, POOL // 2)
    def _(k):
        pl.semaphore_signal(
            barrier, inc=1, device_id={"batch": 1 - b, "pool": 2 * k + core}, device_id_type=MESH
        )

    load_t.start()
    for c in load_kv(7) + load_ids:
        c.start()
    for i in range(1, 8):
        for c in load_kv(near_first(i)):
            c.start()
    for i in range(4):
        load_q(i, 0).start()
        load_q(i, 1).start()

    load_t.wait()

    normed[...] = layer_norm(tokens[...].astype(F32)).astype(BF16)

    for c in load_ids:
        c.wait()
    length = lengths[0]
    row_pos = s * ROWS + lax.broadcasted_iota(jnp.int32, (ROWS, 1), 0)
    row_valid = row_pos < length

    def send_kv(k):
        return remote(
            kvs.at[k], kvr.at[s], kv_sem.at[0, k], kv_sem.at[1, k], seq=(s + k) % SEQ
        )

    def recv_kv(k):
        return remote(
            kvs.at[k], kvr.at[(s + SEQ - k) % SEQ], kv_sem.at[0, k], kv_sem.at[1, k], seq=(s + k) % SEQ
        )

    def make_kv(k):
        for c in load_kv(k):
            c.wait()
        both = silu(dot(normed[...], wkv[k]))
        kvs[k, 0] = both[:, :HEAD].astype(BF16)
        kvs[k, 1] = jnp.where(row_valid, both[:, HEAD:], 0.0).astype(BF16)

    make_kv(7)
    pl.semaphore_wait(barrier, (SEQ - 1) + (POOL - 1) + POOL // 2)
    send_kv(7).start()

    @pl.loop(1, SEQ)
    def _(i):
        k = near_first(i)
        make_kv(k)

        @pl.when(i < SEQ - 1)
        def _():
            send_kv(k).start()

    kvr[s] = kvs[0]
    load_n.start()
    load_pos.start()
    load_g.start()
    load_o.start()
    load_p.start()

    def send_q(k):
        return remote(qs.at[k], qr.at[s], q_sem.at[0, k], q_sem.at[1, k], seq=(s + k) % SEQ)

    def recv_q(k):
        return remote(
            qs.at[k], qr.at[(s + SEQ - k) % SEQ], q_sem.at[0, k], q_sem.at[1, k], seq=(s + k) % SEQ
        )

    @pl.loop(0, SEQ // 2)
    def _(i):
        load_q(i, 0).wait()
        load_q(i, 1).wait()
        both = silu(dot(normed[...], wq[i])).astype(BF16)
        k0 = far_first(2 * i)
        k1 = far_first(2 * i + 1)
        qs[k0] = both[:, :HEAD]
        send_q(k0).start()

        @pl.when(i < SEQ // 2 - 1)
        def _():
            qs[k1] = both[:, HEAD:]
            send_q(k1).start()

        @pl.when(i == SEQ // 2 - 1)
        def _():
            qr[s] = both[:, HEAD:]

    load_n.wait()
    neg = neg_embed[...].astype(F32)
    neg_norm = jnp.sqrt(jnp.sum(neg * neg, axis=-1, keepdims=True) + UNIT_EPSILON)
    neg_unit[...] = neg / neg_norm
    negs[p] = neg_unit[...].astype(BF16)
    ids_all[p] = neg_ids[...]

    def send_ids(k):
        return remote(ids_all.at[p], ids_all.at[p], id_sem.at[0, k], id_sem.at[1, k], pool=(p + k) % POOL)

    def recv_ids(k):
        src = (p + POOL - k) % POOL
        return remote(ids_all.at[src], ids_all.at[src], id_sem.at[0, k], id_sem.at[1, k], pool=src)

    def send_negs(k):
        return remote(negs.at[p], negs.at[p], neg_sem.at[0, k], neg_sem.at[1, k], pool=(p + k) % POOL)

    def recv_negs(k):
        src = (p + POOL - k) % POOL
        return remote(negs.at[src], negs.at[src], neg_sem.at[0, k], neg_sem.at[1, k], pool=src)

    @pl.loop(1, POOL)
    def _(k):
        send_ids(k).start()

    @pl.loop(1, POOL)
    def _(k):
        send_negs(k).start()

    load_g.wait()

    @pl.loop(0, 4)
    def _(i):
        cols = pl.ds(pl.multiple_of(i * 256, 256), 256)
        gate[:, cols] = silu(dot(normed[...], wg[:, cols])).astype(BF16)

    load_pos.wait()
    pos = jnp.transpose(pos_embed[...].astype(F32))
    pos_t[...] = pos / jnp.sqrt(jnp.sum(pos * pos, axis=0, keepdims=True) + UNIT_EPSILON)
    pos_row = pos_ids[...]

    @pl.loop(1, POOL)
    def _(k):
        recv_ids(k).wait_recv()

    ids = jnp.concatenate([ids_all[j] for j in range(POOL)], axis=0)
    factor = jnp.transpose(inverse_chance(ids.astype(F32)))
    ids_col = jnp.transpose(ids.astype(F32)).astype(jnp.int32)
    for j in range(POOL):
        cmask[j] = jnp.where(ids_col[:, j : j + 1] != pos_row, factor[:, j : j + 1], 0.0)

    def half_rows(h):
        return pl.ds(h * HALF, HALF)

    def send_o(k, h):
        return remote(
            osend.at[k, half_rows(h)],
            orecv.at[s, half_rows(h)],
            o_sem.at[h, 0, k],
            o_sem.at[h, 1, k],
            seq=(s + SEQ - k) % SEQ,
        )

    def recv_o(k, h):
        src = (s + k) % SEQ
        return remote(
            osend.at[k, half_rows(h)],
            orecv.at[src, half_rows(h)],
            o_sem.at[h, 0, k],
            o_sem.at[h, 1, k],
            seq=src,
        )

    @pl.loop(1, SEQ)
    def _(k):
        recv_kv(k).wait_recv()

    scale = 0.5 / math.sqrt(HEAD)

    @pl.loop(0, SEQ)
    def _(i):
        k = far_first((i + SEQ - 1) % SEQ)
        a = (s + SEQ - k) % SEQ

        @pl.when(i > 0)
        def _():
            recv_q(k).wait_recv()

        query = qr[a]

        def weights(u):
            half = scale * dot_nt(query, kvr[u, 0])
            return half + half * jnp.tanh(half)

        def group(g, total):
            for u in range(4):
                total = total + dot(weights(4 * g + u).astype(BF16), kvr[4 * g + u, 1])
            return total

        total = lax.fori_loop(0, a // 4, group, jnp.zeros((ROWS, HEAD), F32))
        t_pos = a * ROWS + lax.broadcasted_iota(jnp.int32, (ROWS, ROWS), 0)
        u_pos = lax.broadcasted_iota(jnp.int32, (ROWS, ROWS), 1)
        for last in range(4):
            u = 4 * (a // 4) + last
            seen = jnp.where(u * ROWS + u_pos <= t_pos, weights(u), 0.0).astype(BF16)
            total = total + dot(seen, kvr[u, 1])

        @pl.when(i > 0)
        def _():
            osend[k] = total.astype(BF16)
            send_o(k, 0).start()

        @pl.when(i == 0)
        def _():
            orecv[s] = total.astype(BF16)

    @pl.loop(1, SEQ)
    def _(i):
        send_o(far_first(i - 1), 1).start()

    @pl.loop(1, SEQ)
    def _(k):
        send_kv(k).wait_send()
        send_q(k).wait_send()

    @pl.loop(1, POOL)
    def _(k):
        send_ids(k).wait_send()
        send_negs(k).wait_send()

    @pl.loop(0, POOL)
    def _(k):
        @pl.when(k > 0)
        def _():
            recv_negs(k).wait_recv()

        src = (p + POOL - k) % POOL
        negs_t[:, pl.ds(pl.multiple_of(src * ROWS, ROWS), ROWS)] = jnp.transpose(negs[src])

    load_o.wait()
    load_p.wait()

    @pl.loop(0, 2)
    def _(h):
        start = pl.multiple_of(h * HALF, HALF)
        rows = pl.ds(start, HALF)

        @pl.loop(1, SEQ)
        def _(k):
            recv_o(k, h).wait_recv()

        attn = jnp.concatenate([orecv[j, rows] for j in range(HEADS)], axis=1).astype(F32)
        gated = (layer_norm(attn) * gate[rows, :].astype(F32)).astype(BF16)
        layer_half = (dot(gated, wo[...]) + tokens[rows, :].astype(F32)).astype(BF16)
        layer_out[rows, :] = layer_half
        out = dot(layer_half, wp[...])
        out_hat[rows, :] = (
            out * lax.rsqrt(jnp.sum(out * out, axis=-1, keepdims=True) + UNIT_EPSILON)
        ).astype(BF16)
        out_t = jnp.transpose(out)
        norm_t = jnp.sqrt(jnp.sum(out_t * out_t, axis=0, keepdims=True) + UNIT_EPSILON)
        unit_t = out_t / norm_t
        hat_t = unit_t.astype(BF16)
        pos_half = pos_t[:, rows]
        pos_dot = jnp.sum(hat_t.astype(F32) * pos_half, axis=0, keepdims=True) * (1.0 / WARMTH)
        pos_logit = pos_dot + jnp.log(inverse_chance(pos_ids[:, rows].astype(F32)))
        pos_exp = jnp.exp(pos_logit)

        def scores(j, sums):
            value = jnp.exp(dot(negs[j], hat_t) * (1.0 / WARMTH)) * cmask[j, :, rows]
            kept[j] = value
            return sums + jnp.sum(value, axis=0, keepdims=True)

        total = lax.fori_loop(0, POOL, scores, pos_exp, unroll=8)
        valid = s * ROWS + start + lax.broadcasted_iota(jnp.int32, (1, HALF), 1) < length
        loss[:, rows] = jnp.where(valid, jnp.log(total) - pos_logit, 0.0)
        share = jnp.where(valid, 1.0 / (total * HIST), 0.0)
        pos_weight = jnp.where(valid, pos_exp / total - 1.0, 0.0) * (1.0 / HIST)

        @pl.loop(0, POOL, unroll=4)
        def _(j):
            wt[pl.ds(pl.multiple_of(j * ROWS, ROWS), ROWS), rows] = (kept[j] * share).astype(BF16)

        rows_t = dot(negs_t[...], wt[:, rows])
        grad_t = (pos_weight * pos_half + rows_t) * (1.0 / WARMTH)
        d_out[rows, :] = jnp.transpose(
            (grad_t - unit_t * jnp.sum(unit_t * grad_t, axis=0, keepdims=True)) / norm_t
        ).astype(BF16)

    out_loss = pltpu.make_async_copy(loss, loss_ref, out_sem.at[3])
    out_loss.start()

    half = WIDTH // 2
    mine = pl.ds(pl.multiple_of(core * half, half), half)
    theirs = pl.ds(pl.multiple_of((1 - core) * half, half), half)
    pcs[...] = dot_tn(layer_out[:, theirs], d_out[...]).astype(BF16)
    send_pc = remote(pcs, pcr, pc_sem.at[0], pc_sem.at[1], pool=sibling)
    send_pc.start()
    term[...] = dot_tn(layer_out[:, mine], d_out[...])

    def place(n):
        y_at = (y + 1 + n // 2) % 4
        x_at = xlo + (1 - n % 2) * (1 - 2 * xlo)
        return y_at, x_at

    def send_c(m):
        return remote(cs.at[m], cr.at[m], c_sem.at[0, m], c_sem.at[1, m], pool=sibling)

    def portion(j):
        weight = wt[pl.ds(pl.multiple_of(j * ROWS, ROWS), ROWS), :]
        return dot(weight, out_hat[...]) * (1.0 / WARMTH)

    @pl.loop(0, 4, unroll=2)
    def _(n):
        y_at, x_at = place(n)
        m = 2 * y_at + x_at
        cs[m] = portion(2 * m + 1 - core).astype(BF16)
        send_c(m).start()

    x = 2 * b + xlo

    def plane(n, sign):
        dx, dy = STEPS[n]
        x_at = (x + (dx if sign > 0 else 4 - dx)) % 4
        y_at = (y + (dy if sign > 0 else 4 - dy)) % 4
        q = (x_at // 2) * 8 + y_at * 2 + x_at % 2
        return q, {"batch": x_at // 2, "pool": y_at * 4 + (x_at % 2) * 2 + core}

    def send_px(n):
        q, device = plane(n, 1)
        return remote(
            pxs.at[pl.ds(pl.multiple_of(q * 32, 32), 32), :],
            pxr.at[q_own],
            px_sem.at[0, n],
            px_sem.at[1, n],
            **device,
        )

    def recv_px(n):
        q, device = plane(n, -1)
        return remote(pxs.at[pl.ds(0, 32), :], pxr.at[q], px_sem.at[0, n], px_sem.at[1, n], **device)

    send_pc.wait_recv()
    pxs[...] = (term[...] + pcr[...].astype(F32)).astype(BF16)
    for n in range(GRID - 1):
        send_px(n).start()

    @pl.loop(4, 8, unroll=2)
    def _(n):
        y_at, x_at = place(n)
        m = 2 * y_at + x_at
        cs[m] = portion(2 * m + 1 - core).astype(BF16)
        send_c(m).start()

    pxr[q_own] = pxs[pl.ds(pl.multiple_of(q_own * 32, 32), 32), :]

    def send_x(i):
        return remote(xs.at[i], xr.at[i], x_sem.at[0, i], x_sem.at[1, i], pool=across)

    def send_yb(k):
        return remote(
            ybs.at[k], ybr.at[k], yb_sem.at[0, k], yb_sem.at[1, k], pool=((y + k) % 4) * 4 + p % 4
        )

    @pl.loop(0, 4)
    def _(n):
        y_at = (y + 1 + n) % 4
        m_far = 2 * y_at + 1 - xlo
        m_near = 2 * y_at + xlo
        far = portion(2 * m_far + core)
        near = portion(2 * m_near + core)
        send_c(m_far).wait_recv()
        far = far + cr[m_far].astype(F32)
        xs[y_at] = far[:HALF].astype(BF16)
        send_x(y_at).start()
        send_c(m_near).wait_recv()
        near = near + cr[m_near].astype(F32)
        own[m_near] = near

        @pl.when(n < 3)
        def _():
            ybs[1 + n, 1 - xlo] = far[HALF:].astype(BF16)
            ybs[1 + n, xlo] = near[HALF:].astype(BF16)
            send_yb(1 + n).start()

        @pl.when(n == 3)
        def _():
            own[m_far] = far

    def send_pz(k):
        return remote(pzr.at[s], pzr.at[s], pz_sem.at[0, k], pz_sem.at[1, k], seq=(s + k) % SEQ)

    def recv_pz(k):
        src = (s + SEQ - k) % SEQ
        return remote(pzr.at[src], pzr.at[src], pz_sem.at[0, k], pz_sem.at[1, k], seq=src)

    for n in range(GRID - 1):
        recv_px(n).wait_recv()

    block = pxr[0].astype(F32)
    for q in range(1, GRID):
        block = block + pxr[q].astype(F32)
    pzr[s] = block.astype(BF16)

    @pl.loop(0, SEQ - 1)
    def _(i):
        send_pz(far_first(i)).start()

    @pl.loop(1, SEQ)
    def _(k):
        send_o(k, 0).wait_send()
        send_o(k, 1).wait_send()

    @pl.loop(0, 8)
    def _(m):
        send_c(m).wait_send()

    send_pc.wait_send()
    for n in range(GRID - 1):
        send_px(n).wait_send()

    def send_y(k):
        return remote(
            ys.at[k], yr.at[k], y_sem.at[0, k], y_sem.at[1, k], pool=((y + k) % 4) * 4 + p % 4
        )

    send_xb = remote(xbs, xbr, xb_sem.at[0], xb_sem.at[1], pool=across)

    @pl.loop(1, 4)
    def _(k):
        i = (y + k) % 4
        send_x(i).wait_recv()
        ys[k] = (own[2 * i + xlo, :128] + xr[i].astype(F32)).astype(BF16)
        send_y(k).start()

    lower_theirs = own[2 * y + 1 - xlo, 128:]
    lower = own[2 * y + xlo, 128:]
    for k in range(1, 4):
        send_yb(k).wait_recv()
        lower_theirs = lower_theirs + ybr[k, 1 - xlo].astype(F32)
        lower = lower + ybr[k, xlo].astype(F32)
    xbs[...] = lower_theirs.astype(BF16)
    send_xb.start()
    send_x(y).wait_recv()
    own[2 * y + xlo, :128] = own[2 * y + xlo, :128] + xr[y].astype(F32)
    own[2 * y + xlo, 128:] = lower

    @pl.loop(0, 4)
    def _(i):
        send_x(i).wait_send()

    @pl.loop(1, 4)
    def _(k):
        send_yb(k).wait_send()

    @pl.loop(1, SEQ)
    def _(k):
        recv_pz(k).wait_recv()

    whole = pzr[0].astype(F32)
    for z in range(1, SEQ):
        whole = whole + pzr[z].astype(F32)
    fin[core * GRID + q_own] = whole.astype(BF16)

    def send_f(n):
        at = core * GRID + q_own
        return remote(fin.at[at], fin.at[at], f_sem.at[0, n], f_sem.at[1, n], **plane(n, 1)[1])

    def recv_f(n):
        q, device = plane(n, -1)
        at = core * GRID + q
        return remote(fin.at[at], fin.at[at], f_sem.at[0, n], f_sem.at[1, n], **device)

    ours = fin.at[pl.ds(core * GRID, GRID)]
    others = fin.at[pl.ds((1 - core) * GRID, GRID)]
    send_fc = remote(ours, ours, fc_sem.at[0], fc_sem.at[1], pool=sibling)
    recv_fc = remote(others, others, fc_sem.at[0], fc_sem.at[1], pool=sibling)
    out_ours = pltpu.make_async_copy(ours, dproj_ref.at[pl.ds(core * GRID, GRID)], out_sem.at[0])
    out_others = pltpu.make_async_copy(
        others, dproj_ref.at[pl.ds((1 - core) * GRID, GRID)], out_sem.at[1]
    )

    for n in range(GRID - 1):
        send_f(n).start()

    def send_z(h, k):
        return remote(
            zs.at[h, k], zr.at[h, k], z_sem.at[h, 0, k], z_sem.at[h, 1, k], seq=(s + k) % SEQ
        )

    def project(h, neg_sum):
        rows = slice(h * HALF, (h + 1) * HALF)
        neg = neg_embed[rows, :].astype(F32)
        neg_norm = jnp.sqrt(jnp.sum(neg * neg, axis=-1, keepdims=True) + UNIT_EPSILON)
        unit = neg_unit[rows, :]
        neg_t[:, rows] = jnp.transpose(
            (neg_sum - unit * jnp.sum(unit * neg_sum, axis=-1, keepdims=True)) / neg_norm
        )

        @pl.loop(0, SEQ - 1)
        def _(i):
            k = far_first(i)
            cols = pl.ds(pl.multiple_of(((s + k) % SEQ) * 32, 32), 32)
            zs[h, k] = neg_t[cols, rows].astype(BF16)
            send_z(h, k).start()

    send_xb.wait_recv()
    project(1, own[2 * y + xlo, HALF:] + xbr[...].astype(F32))
    upper = own[2 * y + xlo, :HALF]
    for k in range(1, 4):
        send_y(k).wait_recv()
        upper = upper + yr[k].astype(F32)
    project(0, upper)

    @pl.loop(1, SEQ)
    def _(k):
        send_pz(k).wait_send()

    @pl.loop(1, 4)
    def _(k):
        send_y(k).wait_send()

    send_xb.wait_send()

    for n in range(GRID - 1):
        recv_f(n).wait_recv()
    send_fc.start()
    out_ours.start()
    for n in range(GRID - 1):
        send_f(n).wait_send()

    for h in (1, 0):
        rows = slice(h * HALF, (h + 1) * HALF)
        part = neg_t[pl.ds(pl.multiple_of(s * 32, 32), 32), rows]
        for k in range(1, SEQ):
            send_z(h, k).wait_recv()
            part = part + zr[h, k].astype(F32)
        dneg[:, rows] = part
    out_dneg = pltpu.make_async_copy(dneg, dneg_ref, out_sem.at[2])
    out_dneg.start()

    recv_fc.wait_recv()
    out_others.start()

    @pl.loop(1, SEQ)
    def _(k):
        send_z(0, k).wait_send()
        send_z(1, k).wait_send()

    send_fc.wait_send()
    out_loss.wait()
    out_dneg.wait()
    out_ours.wait()
    out_others.wait()


def finish(loss, dneg_t, dproj, loss_out, dneg_out, dproj_out, narrow, wide, sem):
    rows = WIDTH // 4
    loss_copy = pltpu.make_async_copy(loss, loss_out, sem.at[8])
    dneg_copy = pltpu.make_async_copy(dneg_t, dneg_out, sem.at[9])
    loads = [
        pltpu.make_async_copy(dproj.at[pl.ds(c * rows, rows)], narrow.at[c], sem.at[c]) for c in range(4)
    ]
    stores = [
        pltpu.make_async_copy(wide.at[c], dproj_out.at[pl.ds(c * rows, rows)], sem.at[4 + c])
        for c in range(4)
    ]
    for load in loads:
        load.start()
    loss_copy.start()
    dneg_copy.start()
    for c in range(4):
        loads[c].wait()
        wide[c] = narrow[c].astype(F32)
        stores[c].start()
    for store in stores:
        store.wait()
    loss_copy.wait()
    dneg_copy.wait()


def body(tokens, w_in, w_out, w_proj, pos_embed, pos_ids, lengths, neg_embed, neg_ids):
    hbm = pl.BlockSpec(memory_space=pl.ANY)
    dma = pltpu.SemaphoreType.DMA
    loss, dneg_t, dproj = pl.pallas_call(
        kernel,
        out_shape=(
            jax.ShapeDtypeStruct((1, ROWS), F32),
            jax.ShapeDtypeStruct((EMBED // SEQ, ROWS), F32),
            jax.ShapeDtypeStruct((2 * GRID, 32, EMBED), BF16),
        ),
        in_specs=[hbm] * 9,
        out_specs=(hbm, hbm, hbm),
        scratch_shapes=[
            pltpu.VMEM((ROWS, WIDTH), BF16),
            pltpu.VMEM((ROWS, EMBED), BF16),
            pltpu.VMEM((ROWS, EMBED), BF16),
            pltpu.VMEM((1, ROWS), jnp.int32),
            pltpu.VMEM((1, ROWS), jnp.int32),
            pltpu.SMEM((1,), jnp.int32),
            pltpu.VMEM((8, WIDTH, 256), BF16),
            pltpu.VMEM((4, WIDTH, 256), BF16),
            pltpu.VMEM((WIDTH, WIDTH), BF16),
            pltpu.VMEM((WIDTH, WIDTH), BF16),
            pltpu.VMEM((WIDTH, EMBED), BF16),
            pltpu.VMEM((ROWS, WIDTH), BF16),
            pltpu.VMEM((SEQ, 2, ROWS, HEAD), BF16),
            pltpu.VMEM((SEQ, 2, ROWS, HEAD), BF16),
            pltpu.VMEM((SEQ, ROWS, HEAD), BF16),
            pltpu.VMEM((SEQ, ROWS, HEAD), BF16),
            pltpu.VMEM((SEQ, ROWS, HEAD), BF16),
            pltpu.VMEM((SEQ, ROWS, HEAD), BF16),
            pltpu.VMEM((ROWS, WIDTH), BF16),
            pltpu.VMEM((POOL, ROWS, EMBED), BF16),
            pltpu.VMEM((EMBED, POOL * ROWS), BF16),
            pltpu.VMEM((POOL, 1, ROWS), jnp.int32),
            pltpu.VMEM((POOL, ROWS, ROWS), F32),
            pltpu.VMEM((POOL, ROWS, HALF), F32),
            pltpu.VMEM((POOL * ROWS, ROWS), BF16),
            pltpu.VMEM((ROWS, WIDTH), BF16),
            pltpu.VMEM((ROWS, EMBED), BF16),
            pltpu.VMEM((ROWS, EMBED), BF16),
            pltpu.VMEM((EMBED, ROWS), F32),
            pltpu.VMEM((ROWS, EMBED), F32),
            pltpu.VMEM((8, ROWS, EMBED), BF16),
            pltpu.VMEM((8, ROWS, EMBED), BF16),
            pltpu.VMEM((8, ROWS, EMBED), F32),
            pltpu.VMEM((4, 128, EMBED), BF16),
            pltpu.VMEM((4, 128, EMBED), BF16),
            pltpu.VMEM((4, 128, EMBED), BF16),
            pltpu.VMEM((4, 128, EMBED), BF16),
            pltpu.VMEM((4, 2, 128, EMBED), BF16),
            pltpu.VMEM((4, 2, 128, EMBED), BF16),
            pltpu.VMEM((128, EMBED), BF16),
            pltpu.VMEM((128, EMBED), BF16),
            pltpu.VMEM((EMBED, ROWS), F32),
            pltpu.VMEM((2, SEQ, 32, HALF), BF16),
            pltpu.VMEM((2, SEQ, 32, HALF), BF16),
            pltpu.VMEM((WIDTH // 2, EMBED), F32),
            pltpu.VMEM((WIDTH // 2, EMBED), BF16),
            pltpu.VMEM((WIDTH // 2, EMBED), BF16),
            pltpu.VMEM((WIDTH // 2, EMBED), BF16),
            pltpu.VMEM((GRID, 32, EMBED), BF16),
            pltpu.VMEM((SEQ, 32, EMBED), BF16),
            pltpu.VMEM((2 * GRID, 32, EMBED), BF16),
            pltpu.VMEM((1, ROWS), F32),
            pltpu.VMEM((EMBED // SEQ, ROWS), F32),
            dma((33,)),
            dma((2, SEQ)),
            dma((2, SEQ)),
            dma((2, 2, SEQ)),
            dma((2, POOL)),
            dma((2, POOL)),
            dma((2, 8)),
            dma((2, 4)),
            dma((2, 4)),
            dma((2, 4)),
            dma((2,)),
            dma((2, 2, SEQ)),
            dma((2,)),
            dma((2, GRID)),
            dma((2, SEQ)),
            dma((2, GRID)),
            dma((2,)),
            dma((4,)),
        ],
        compiler_params=pltpu.CompilerParams(
            collective_id=0, has_side_effects=True, vmem_limit_bytes=56 * 1024 * 1024
        ),
    )(
        tokens[0],
        w_in,
        w_out,
        w_proj,
        pos_embed[0],
        pos_ids,
        lengths,
        neg_embed[0],
        neg_ids,
    )
    loss, dneg_t, dproj = pl.pallas_call(
        finish,
        out_shape=(
            jax.ShapeDtypeStruct((1, ROWS), F32),
            jax.ShapeDtypeStruct((EMBED // SEQ, ROWS), F32),
            jax.ShapeDtypeStruct((WIDTH, EMBED), F32),
        ),
        in_specs=[hbm] * 3,
        out_specs=(hbm, hbm, hbm),
        scratch_shapes=[
            pltpu.VMEM((4, WIDTH // 4, EMBED), BF16),
            pltpu.VMEM((4, WIDTH // 4, EMBED), F32),
            dma((10,)),
        ],
    )(loss, dneg_t, dproj.reshape(WIDTH, EMBED))
    return (loss, jnp.transpose(dneg_t)[None], dproj)


def solution(mesh):
    placed = (
        P(("batch", "pool"), "seq", None),
        P(),
        P(),
        P(),
        P(("batch", "pool"), "seq", None),
        P(("batch", "pool"), "seq"),
        P(("batch", "pool")),
        P("batch", "pool", None),
        P("batch", "pool"),
    )
    return jax.shard_map(
        body,
        mesh=mesh,
        in_specs=placed,
        out_specs=(P(("batch", "pool"), "seq"), P("batch", "pool", "seq"), P()),
        check_vma=False,
    )
```

```python
import math

import jax
import jax.numpy as jnp
from jax import lax
from jax.experimental import pallas as pl
from jax.experimental.pallas import tpu as pltpu
from jax.sharding import PartitionSpec as P

HEADS = 8
HEAD = 128
ROWS = 256
HALF = 128
WIDTH = 1024
EMBED = 256
SEQ = 8
POOL = 16
BATCH = 2
GRID = 16
ITEMS = 1048576
HIST = 32
WARMTH = 0.02
NORM_EPSILON = 1e-05
UNIT_EPSILON = 1e-06
MESH = pl.DeviceIdType.MESH
F32 = jnp.float32
BF16 = jnp.bfloat16


def dot(a, b):
    return jnp.dot(a, b, preferred_element_type=F32)


def dot_nt(a, b):
    return lax.dot_general(a, b, (((1,), (1,)), ((), ())), preferred_element_type=F32)


def dot_tn(a, b):
    return lax.dot_general(a, b, (((0,), (0,)), ((), ())), preferred_element_type=F32)


def silu(v):
    half = 0.5 * v
    return half + half * jnp.tanh(half)


def layer_norm(inputs):
    center = inputs - jnp.mean(inputs, axis=-1, keepdims=True)
    spread = jnp.mean(center * center, axis=-1, keepdims=True)
    return center * lax.rsqrt(spread + NORM_EPSILON)


def inverse_chance(ids):
    z = 1.0 / (2.0 * ids + 3.0)
    z2 = z * z
    series = 1.0 / 17.0
    for odd in (15, 13, 11, 9, 7, 5, 3, 1):
        series = series * z2 + 1.0 / odd
    return math.log(ITEMS + 1.0) / (2.0 * z * series)


STEPS = sorted(
    [(dx, dy) for dx in range(4) for dy in range(4) if dx or dy],
    key=lambda d: -(min(d[0], 4 - d[0]) + min(d[1], 4 - d[1])),
)


def far_first(i):
    return 4 + (1 - 2 * (i % 2)) * ((i + 1) // 2)


def far_y(n):
    return 2 + (1 - 2 * (n % 2)) * ((n + 1) // 2)


def near_first(i):
    return far_first((14 - i) % 8)


def remote(src, dst, send, recv, **device):
    return pltpu.make_async_remote_copy(
        src_ref=src, dst_ref=dst, send_sem=send, recv_sem=recv, device_id=device, device_id_type=MESH
    )


def kernel(
    tokens_hbm,
    w_in,
    w_out,
    w_proj,
    pos_hbm,
    pos_ids_hbm,
    lengths_hbm,
    neg_hbm,
    neg_ids_hbm,
    loss_ref,
    dneg_ref,
    dproj_ref,
    tokens,
    pos_embed,
    neg_embed,
    pos_ids,
    neg_ids,
    lengths,
    wkv,
    wq,
    wg,
    wo,
    wp,
    normed,
    kvs,
    kvr,
    qs,
    qr,
    osend,
    orecv,
    gate,
    negs,
    negs_t,
    ids_all,
    cmask,
    kept,
    wt,
    layer_out,
    out_hat,
    d_out,
    pos_t,
    neg_unit,
    cs,
    cr,
    own,
    xs,
    xr,
    ys,
    yr,
    ybs,
    ybr,
    xbs,
    xbr,
    neg_t,
    zs,
    zr,
    term,
    pcs,
    pcr,
    pxs,
    pxr,
    pzr,
    fin,
    loss,
    dneg,
    w_sem,
    kv_sem,
    q_sem,
    o_sem,
    neg_sem,
    id_sem,
    c_sem,
    x_sem,
    y_sem,
    yb_sem,
    xb_sem,
    z_sem,
    pc_sem,
    px_sem,
    pz_sem,
    f_sem,
    fc_sem,
    out_sem,
):
    b = lax.axis_index("batch")
    s = lax.axis_index("seq")
    p = lax.axis_index("pool")
    core = p % 2
    xlo = (p // 2) % 2
    y = p // 4
    sibling = p + 1 - 2 * core
    across = p + 2 - 4 * xlo
    q_own = b * 8 + p // 2

    load_ids = [
        pltpu.make_async_copy(pos_ids_hbm, pos_ids, w_sem.at[30]),
        pltpu.make_async_copy(neg_ids_hbm, neg_ids, w_sem.at[31]),
        pltpu.make_async_copy(lengths_hbm, lengths, w_sem.at[32]),
    ]
    def load_kv(k):
        h = (s + k) % SEQ
        return [
            pltpu.make_async_copy(
                w_in.at[:, pl.ds(pl.multiple_of(3 * WIDTH + h * HEAD, HEAD), HEAD)],
                wkv.at[k, :, pl.ds(0, HEAD)],
                w_sem.at[k],
            ),
            pltpu.make_async_copy(
                w_in.at[:, pl.ds(pl.multiple_of(WIDTH + h * HEAD, HEAD), HEAD)],
                wkv.at[k, :, pl.ds(HEAD, HEAD)],
                w_sem.at[8 + k],
            ),
        ]

    def load_q(i, half):
        h = (s + far_first(2 * i + half)) % SEQ
        return pltpu.make_async_copy(
            w_in.at[:, pl.ds(pl.multiple_of(2 * WIDTH + h * HEAD, HEAD), HEAD)],
            wq.at[i, :, pl.ds(half * HEAD, HEAD)],
            w_sem.at[16 + 2 * i + half],
        )

    load_g = pltpu.make_async_copy(w_in.at[:, pl.ds(0, WIDTH)], wg, w_sem.at[24])
    load_o = pltpu.make_async_copy(w_out, wo, w_sem.at[25])
    load_p = pltpu.make_async_copy(w_proj, wp, w_sem.at[26])
    load_t = pltpu.make_async_copy(tokens_hbm, tokens, w_sem.at[27])
    load_n = pltpu.make_async_copy(neg_hbm, neg_embed, w_sem.at[28])
    load_pos = pltpu.make_async_copy(pos_hbm, pos_embed, w_sem.at[29])
    barrier = pltpu.get_barrier_semaphore()

    @pl.loop(1, SEQ)
    def _(k):
        pl.semaphore_signal(barrier, inc=1, device_id={"seq": (s + k) % SEQ}, device_id_type=MESH)

    @pl.loop(1, POOL)
    def _(k):
        pl.semaphore_signal(barrier, inc=1, device_id={"pool": (p + k) % POOL}, device_id_type=MESH)

    @pl.loop(0, POOL // 2)
    def _(k):
        pl.semaphore_signal(
            barrier, inc=1, device_id={"batch": 1 - b, "pool": 2 * k + core}, device_id_type=MESH
        )

    load_t.start()
    for c in load_kv(7) + load_ids:
        c.start()
    for i in range(1, 8):
        for c in load_kv(near_first(i)):
            c.start()
    for i in range(4):
        load_q(i, 0).start()
        load_q(i, 1).start()

    load_t.wait()

    normed[...] = layer_norm(tokens[...].astype(F32)).astype(BF16)

    for c in load_ids:
        c.wait()
    length = lengths[0]
    row_pos = s * ROWS + lax.broadcasted_iota(jnp.int32, (ROWS, 1), 0)
    row_valid = row_pos < length

    def send_kv(k):
        return remote(
            kvs.at[k], kvr.at[s], kv_sem.at[0, k], kv_sem.at[1, k], seq=(s + k) % SEQ
        )

    def recv_kv(k):
        return remote(
            kvs.at[k], kvr.at[(s + SEQ - k) % SEQ], kv_sem.at[0, k], kv_sem.at[1, k], seq=(s + k) % SEQ
        )

    def make_kv(k):
        for c in load_kv(k):
            c.wait()
        both = silu(dot(normed[...], wkv[k]))
        kvs[k, 0] = both[:, :HEAD].astype(BF16)
        kvs[k, 1] = jnp.where(row_valid, both[:, HEAD:], 0.0).astype(BF16)

    make_kv(7)
    pl.semaphore_wait(barrier, (SEQ - 1) + (POOL - 1) + POOL // 2)
    send_kv(7).start()

    @pl.loop(1, SEQ)
    def _(i):
        k = near_first(i)
        make_kv(k)

        @pl.when(i < SEQ - 1)
        def _():
            send_kv(k).start()

    kvr[s] = kvs[0]
    load_n.start()
    load_pos.start()
    load_g.start()
    load_o.start()
    load_p.start()

    def send_q(k):
        return remote(qs.at[k], qr.at[s], q_sem.at[0, k], q_sem.at[1, k], seq=(s + k) % SEQ)

    def recv_q(k):
        return remote(
            qs.at[k], qr.at[(s + SEQ - k) % SEQ], q_sem.at[0, k], q_sem.at[1, k], seq=(s + k) % SEQ
        )

    @pl.loop(0, SEQ // 2)
    def _(i):
        load_q(i, 0).wait()
        load_q(i, 1).wait()
        both = silu(dot(normed[...], wq[i])).astype(BF16)
        k0 = far_first(2 * i)
        k1 = far_first(2 * i + 1)
        qs[k0] = both[:, :HEAD]
        send_q(k0).start()

        @pl.when(i < SEQ // 2 - 1)
        def _():
            qs[k1] = both[:, HEAD:]
            send_q(k1).start()

        @pl.when(i == SEQ // 2 - 1)
        def _():
            qr[s] = both[:, HEAD:]

    load_n.wait()
    neg = neg_embed[...].astype(F32)
    neg_norm = jnp.sqrt(jnp.sum(neg * neg, axis=-1, keepdims=True) + UNIT_EPSILON)
    neg_unit[...] = neg / neg_norm
    negs[p] = neg_unit[...].astype(BF16)
    ids_all[p] = neg_ids[...]

    def send_ids(k):
        return remote(ids_all.at[p], ids_all.at[p], id_sem.at[0, k], id_sem.at[1, k], pool=(p + k) % POOL)

    def recv_ids(k):
        src = (p + POOL - k) % POOL
        return remote(ids_all.at[src], ids_all.at[src], id_sem.at[0, k], id_sem.at[1, k], pool=src)

    def send_negs(k):
        return remote(negs.at[p], negs.at[p], neg_sem.at[0, k], neg_sem.at[1, k], pool=(p + k) % POOL)

    def recv_negs(k):
        src = (p + POOL - k) % POOL
        return remote(negs.at[src], negs.at[src], neg_sem.at[0, k], neg_sem.at[1, k], pool=src)

    @pl.loop(1, POOL)
    def _(k):
        send_ids(k).start()

    @pl.loop(1, POOL)
    def _(k):
        send_negs(k).start()

    load_g.wait()

    @pl.loop(0, 4)
    def _(i):
        cols = pl.ds(pl.multiple_of(i * 256, 256), 256)
        gate[:, cols] = silu(dot(normed[...], wg[:, cols])).astype(BF16)

    load_pos.wait()
    pos = jnp.transpose(pos_embed[...].astype(F32))
    pos_t[...] = pos / jnp.sqrt(jnp.sum(pos * pos, axis=0, keepdims=True) + UNIT_EPSILON)
    pos_row = pos_ids[...]

    @pl.loop(1, POOL)
    def _(k):
        recv_ids(k).wait_recv()

    ids = jnp.concatenate([ids_all[j] for j in range(POOL)], axis=0)
    factor = jnp.transpose(inverse_chance(ids.astype(F32)))
    ids_col = jnp.transpose(ids.astype(F32)).astype(jnp.int32)
    for j in range(POOL):
        cmask[j] = jnp.where(ids_col[:, j : j + 1] != pos_row, factor[:, j : j + 1], 0.0)

    def half_rows(h):
        return pl.ds(h * HALF, HALF)

    def send_o(k, h):
        return remote(
            osend.at[k, half_rows(h)],
            orecv.at[s, half_rows(h)],
            o_sem.at[h, 0, k],
            o_sem.at[h, 1, k],
            seq=(s + SEQ - k) % SEQ,
        )

    def recv_o(k, h):
        src = (s + k) % SEQ
        return remote(
            osend.at[k, half_rows(h)],
            orecv.at[src, half_rows(h)],
            o_sem.at[h, 0, k],
            o_sem.at[h, 1, k],
            seq=src,
        )

    @pl.loop(1, SEQ)
    def _(k):
        recv_kv(k).wait_recv()

    scale = 0.5 / math.sqrt(HEAD)

    @pl.loop(0, SEQ)
    def _(i):
        k = far_first((i + SEQ - 1) % SEQ)
        a = (s + SEQ - k) % SEQ

        @pl.when(i > 0)
        def _():
            recv_q(k).wait_recv()

        query = qr[a]

        def weights(u):
            half = scale * dot_nt(query, kvr[u, 0])
            return half + half * jnp.tanh(half)

        def group(g, total):
            for u in range(4):
                total = total + dot(weights(4 * g + u).astype(BF16), kvr[4 * g + u, 1])
            return total

        total = lax.fori_loop(0, a // 4, group, jnp.zeros((ROWS, HEAD), F32))
        t_pos = a * ROWS + lax.broadcasted_iota(jnp.int32, (ROWS, ROWS), 0)
        u_pos = lax.broadcasted_iota(jnp.int32, (ROWS, ROWS), 1)
        for last in range(4):
            u = 4 * (a // 4) + last
            seen = jnp.where(u * ROWS + u_pos <= t_pos, weights(u), 0.0).astype(BF16)
            total = total + dot(seen, kvr[u, 1])

        @pl.when(i > 0)
        def _():
            osend[k] = total.astype(BF16)
            send_o(k, 0).start()

        @pl.when(i == 0)
        def _():
            orecv[s] = total.astype(BF16)

    @pl.loop(1, SEQ)
    def _(i):
        send_o(far_first(i - 1), 1).start()

    @pl.loop(1, SEQ)
    def _(k):
        send_kv(k).wait_send()
        send_q(k).wait_send()

    @pl.loop(1, POOL)
    def _(k):
        send_ids(k).wait_send()
        send_negs(k).wait_send()

    @pl.loop(0, POOL)
    def _(k):
        @pl.when(k > 0)
        def _():
            recv_negs(k).wait_recv()

        src = (p + POOL - k) % POOL
        negs_t[:, pl.ds(pl.multiple_of(src * ROWS, ROWS), ROWS)] = jnp.transpose(negs[src])

    load_o.wait()
    load_p.wait()

    @pl.loop(0, 2)
    def _(h):
        start = pl.multiple_of(h * HALF, HALF)
        rows = pl.ds(start, HALF)

        @pl.loop(1, SEQ)
        def _(k):
            recv_o(k, h).wait_recv()

        attn = jnp.concatenate([orecv[j, rows] for j in range(HEADS)], axis=1).astype(F32)
        gated = (layer_norm(attn) * gate[rows, :].astype(F32)).astype(BF16)
        layer_half = (dot(gated, wo[...]) + tokens[rows, :].astype(F32)).astype(BF16)
        layer_out[rows, :] = layer_half
        out = dot(layer_half, wp[...])
        out_hat[rows, :] = (
            out * lax.rsqrt(jnp.sum(out * out, axis=-1, keepdims=True) + UNIT_EPSILON)
        ).astype(BF16)
        out_t = jnp.transpose(out)
        norm_t = jnp.sqrt(jnp.sum(out_t * out_t, axis=0, keepdims=True) + UNIT_EPSILON)
        unit_t = out_t / norm_t
        hat_t = unit_t.astype(BF16)
        pos_half = pos_t[:, rows]
        pos_dot = jnp.sum(hat_t.astype(F32) * pos_half, axis=0, keepdims=True) * (1.0 / WARMTH)
        pos_logit = pos_dot + jnp.log(inverse_chance(pos_ids[:, rows].astype(F32)))
        pos_exp = jnp.exp(pos_logit)

        def scores(j, sums):
            value = jnp.exp(dot(negs[j], hat_t) * (1.0 / WARMTH)) * cmask[j, :, rows]
            kept[j] = value
            return sums + jnp.sum(value, axis=0, keepdims=True)

        total = lax.fori_loop(0, POOL, scores, pos_exp, unroll=8)
        valid = s * ROWS + start + lax.broadcasted_iota(jnp.int32, (1, HALF), 1) < length
        loss[:, rows] = jnp.where(valid, jnp.log(total) - pos_logit, 0.0)
        share = jnp.where(valid, 1.0 / (total * HIST), 0.0)
        pos_weight = jnp.where(valid, pos_exp / total - 1.0, 0.0) * (1.0 / HIST)

        @pl.loop(0, POOL, unroll=4)
        def _(j):
            wt[pl.ds(pl.multiple_of(j * ROWS, ROWS), ROWS), rows] = (kept[j] * share).astype(BF16)

        rows_t = dot(negs_t[...], wt[:, rows])
        grad_t = (pos_weight * pos_half + rows_t) * (1.0 / WARMTH)
        d_out[rows, :] = jnp.transpose(
            (grad_t - unit_t * jnp.sum(unit_t * grad_t, axis=0, keepdims=True)) / norm_t
        ).astype(BF16)

    out_loss = pltpu.make_async_copy(loss, loss_ref, out_sem.at[3])
    out_loss.start()

    half = WIDTH // 2
    mine = pl.ds(pl.multiple_of(core * half, half), half)
    theirs = pl.ds(pl.multiple_of((1 - core) * half, half), half)
    pcs[...] = dot_tn(layer_out[:, theirs], d_out[...]).astype(BF16)
    send_pc = remote(pcs, pcr, pc_sem.at[0], pc_sem.at[1], pool=sibling)
    send_pc.start()
    term[...] = dot_tn(layer_out[:, mine], d_out[...])

    def place(n):
        y_at = (y + far_y(n // 2)) % 4
        x_at = xlo + (1 - n % 2) * (1 - 2 * xlo)
        return y_at, x_at

    def send_c(m):
        return remote(cs.at[m], cr.at[m], c_sem.at[0, m], c_sem.at[1, m], pool=sibling)

    def portion(j):
        weight = wt[pl.ds(pl.multiple_of(j * ROWS, ROWS), ROWS), :]
        return dot(weight, out_hat[...]) * (1.0 / WARMTH)

    @pl.loop(0, 4, unroll=2)
    def _(n):
        y_at, x_at = place(n)
        m = 2 * y_at + x_at
        cs[m] = portion(2 * m + 1 - core).astype(BF16)
        send_c(m).start()

    x = 2 * b + xlo

    def plane(n, sign):
        dx, dy = STEPS[n]
        x_at = (x + (dx if sign > 0 else 4 - dx)) % 4
        y_at = (y + (dy if sign > 0 else 4 - dy)) % 4
        q = (x_at // 2) * 8 + y_at * 2 + x_at % 2
        return q, {"batch": x_at // 2, "pool": y_at * 4 + (x_at % 2) * 2 + core}

    def send_px(n):
        q, device = plane(n, 1)
        return remote(
            pxs.at[pl.ds(pl.multiple_of(q * 32, 32), 32), :],
            pxr.at[q_own],
            px_sem.at[0, n],
            px_sem.at[1, n],
            **device,
        )

    def recv_px(n):
        q, device = plane(n, -1)
        return remote(pxs.at[pl.ds(0, 32), :], pxr.at[q], px_sem.at[0, n], px_sem.at[1, n], **device)

    send_pc.wait_recv()
    pxs[...] = (term[...] + pcr[...].astype(F32)).astype(BF16)
    for n in range(GRID - 1):
        send_px(n).start()

    @pl.loop(4, 8, unroll=2)
    def _(n):
        y_at, x_at = place(n)
        m = 2 * y_at + x_at
        cs[m] = portion(2 * m + 1 - core).astype(BF16)
        send_c(m).start()

    pxr[q_own] = pxs[pl.ds(pl.multiple_of(q_own * 32, 32), 32), :]

    def send_x(i):
        return remote(xs.at[i], xr.at[i], x_sem.at[0, i], x_sem.at[1, i], pool=across)

    def send_yb(k):
        return remote(
            ybs.at[k], ybr.at[k], yb_sem.at[0, k], yb_sem.at[1, k], pool=((y + k) % 4) * 4 + p % 4
        )

    @pl.loop(0, 4)
    def _(n):
        k = far_y(n)
        y_at = (y + k) % 4
        m_far = 2 * y_at + 1 - xlo
        m_near = 2 * y_at + xlo
        far = portion(2 * m_far + core)
        near = portion(2 * m_near + core)
        send_c(m_far).wait_recv()
        far = far + cr[m_far].astype(F32)
        xs[y_at] = far[:HALF].astype(BF16)
        send_x(y_at).start()
        send_c(m_near).wait_recv()
        near = near + cr[m_near].astype(F32)
        own[m_near] = near

        @pl.when(n < 3)
        def _():
            ybs[k, 1 - xlo] = far[HALF:].astype(BF16)
            ybs[k, xlo] = near[HALF:].astype(BF16)
            send_yb(k).start()

        @pl.when(n == 3)
        def _():
            own[m_far] = far

    def send_pz(k):
        return remote(pzr.at[s], pzr.at[s], pz_sem.at[0, k], pz_sem.at[1, k], seq=(s + k) % SEQ)

    def recv_pz(k):
        src = (s + SEQ - k) % SEQ
        return remote(pzr.at[src], pzr.at[src], pz_sem.at[0, k], pz_sem.at[1, k], seq=src)

    for n in range(GRID - 1):
        recv_px(n).wait_recv()

    block = pxr[0].astype(F32)
    for q in range(1, GRID):
        block = block + pxr[q].astype(F32)
    pzr[s] = block.astype(BF16)

    @pl.loop(0, SEQ - 1)
    def _(i):
        send_pz(far_first(i)).start()

    @pl.loop(1, SEQ)
    def _(k):
        send_o(k, 0).wait_send()
        send_o(k, 1).wait_send()

    @pl.loop(0, 8)
    def _(m):
        send_c(m).wait_send()

    send_pc.wait_send()
    for n in range(GRID - 1):
        send_px(n).wait_send()

    def send_y(k):
        return remote(
            ys.at[k], yr.at[k], y_sem.at[0, k], y_sem.at[1, k], pool=((y + k) % 4) * 4 + p % 4
        )

    send_xb = remote(xbs, xbr, xb_sem.at[0], xb_sem.at[1], pool=across)

    @pl.loop(0, 3)
    def _(n):
        k = far_y(n)
        i = (y + k) % 4
        send_x(i).wait_recv()
        ys[k] = (own[2 * i + xlo, :128] + xr[i].astype(F32)).astype(BF16)
        send_y(k).start()

    lower_theirs = own[2 * y + 1 - xlo, 128:]
    lower = own[2 * y + xlo, 128:]
    for k in range(1, 4):
        send_yb(k).wait_recv()
        lower_theirs = lower_theirs + ybr[k, 1 - xlo].astype(F32)
        lower = lower + ybr[k, xlo].astype(F32)
    xbs[...] = lower_theirs.astype(BF16)
    send_xb.start()
    send_x(y).wait_recv()
    own[2 * y + xlo, :128] = own[2 * y + xlo, :128] + xr[y].astype(F32)
    own[2 * y + xlo, 128:] = lower

    @pl.loop(0, 4)
    def _(i):
        send_x(i).wait_send()

    @pl.loop(1, 4)
    def _(k):
        send_yb(k).wait_send()

    @pl.loop(1, SEQ)
    def _(k):
        recv_pz(k).wait_recv()

    whole = pzr[0].astype(F32)
    for z in range(1, SEQ):
        whole = whole + pzr[z].astype(F32)
    fin[core * GRID + q_own] = whole.astype(BF16)

    def send_f(n):
        at = core * GRID + q_own
        return remote(fin.at[at], fin.at[at], f_sem.at[0, n], f_sem.at[1, n], **plane(n, 1)[1])

    def recv_f(n):
        q, device = plane(n, -1)
        at = core * GRID + q
        return remote(fin.at[at], fin.at[at], f_sem.at[0, n], f_sem.at[1, n], **device)

    ours = fin.at[pl.ds(core * GRID, GRID)]
    others = fin.at[pl.ds((1 - core) * GRID, GRID)]
    send_fc = remote(ours, ours, fc_sem.at[0], fc_sem.at[1], pool=sibling)
    recv_fc = remote(others, others, fc_sem.at[0], fc_sem.at[1], pool=sibling)
    out_ours = pltpu.make_async_copy(ours, dproj_ref.at[pl.ds(core * GRID, GRID)], out_sem.at[0])
    out_others = pltpu.make_async_copy(
        others, dproj_ref.at[pl.ds((1 - core) * GRID, GRID)], out_sem.at[1]
    )

    for n in range(GRID - 1):
        send_f(n).start()

    def send_z(h, k):
        return remote(
            zs.at[h, k], zr.at[h, k], z_sem.at[h, 0, k], z_sem.at[h, 1, k], seq=(s + k) % SEQ
        )

    def project(h, neg_sum):
        rows = slice(h * HALF, (h + 1) * HALF)
        neg = neg_embed[rows, :].astype(F32)
        neg_norm = jnp.sqrt(jnp.sum(neg * neg, axis=-1, keepdims=True) + UNIT_EPSILON)
        unit = neg_unit[rows, :]
        neg_t[:, rows] = jnp.transpose(
            (neg_sum - unit * jnp.sum(unit * neg_sum, axis=-1, keepdims=True)) / neg_norm
        )

        @pl.loop(0, SEQ - 1)
        def _(i):
            k = far_first(i)
            cols = pl.ds(pl.multiple_of(((s + k) % SEQ) * 32, 32), 32)
            zs[h, k] = neg_t[cols, rows].astype(BF16)
            send_z(h, k).start()

    send_xb.wait_recv()
    project(1, own[2 * y + xlo, HALF:] + xbr[...].astype(F32))
    upper = own[2 * y + xlo, :HALF]
    for k in range(1, 4):
        send_y(k).wait_recv()
        upper = upper + yr[k].astype(F32)
    project(0, upper)

    @pl.loop(1, SEQ)
    def _(k):
        send_pz(k).wait_send()

    @pl.loop(1, 4)
    def _(k):
        send_y(k).wait_send()

    send_xb.wait_send()

    for n in range(GRID - 1):
        recv_f(n).wait_recv()
    send_fc.start()
    out_ours.start()
    for n in range(GRID - 1):
        send_f(n).wait_send()

    for h in (1, 0):
        rows = slice(h * HALF, (h + 1) * HALF)
        part = neg_t[pl.ds(pl.multiple_of(s * 32, 32), 32), rows]
        for k in range(1, SEQ):
            send_z(h, k).wait_recv()
            part = part + zr[h, k].astype(F32)
        dneg[:, rows] = part
    out_dneg = pltpu.make_async_copy(dneg, dneg_ref, out_sem.at[2])
    out_dneg.start()

    recv_fc.wait_recv()
    out_others.start()

    @pl.loop(1, SEQ)
    def _(k):
        send_z(0, k).wait_send()
        send_z(1, k).wait_send()

    send_fc.wait_send()
    out_loss.wait()
    out_dneg.wait()
    out_ours.wait()
    out_others.wait()


def finish(loss, dneg_t, dproj, loss_out, dneg_out, dproj_out, narrow, wide, sem):
    rows = WIDTH // 4
    loss_copy = pltpu.make_async_copy(loss, loss_out, sem.at[8])
    dneg_copy = pltpu.make_async_copy(dneg_t, dneg_out, sem.at[9])
    loads = [
        pltpu.make_async_copy(dproj.at[pl.ds(c * rows, rows)], narrow.at[c], sem.at[c]) for c in range(4)
    ]
    stores = [
        pltpu.make_async_copy(wide.at[c], dproj_out.at[pl.ds(c * rows, rows)], sem.at[4 + c])
        for c in range(4)
    ]
    for load in loads:
        load.start()
    loss_copy.start()
    dneg_copy.start()
    for c in range(4):
        loads[c].wait()
        wide[c] = narrow[c].astype(F32)
        stores[c].start()
    for store in stores:
        store.wait()
    loss_copy.wait()
    dneg_copy.wait()


def body(tokens, w_in, w_out, w_proj, pos_embed, pos_ids, lengths, neg_embed, neg_ids):
    hbm = pl.BlockSpec(memory_space=pl.ANY)
    dma = pltpu.SemaphoreType.DMA
    loss, dneg_t, dproj = pl.pallas_call(
        kernel,
        out_shape=(
            jax.ShapeDtypeStruct((1, ROWS), F32),
            jax.ShapeDtypeStruct((EMBED // SEQ, ROWS), F32),
            jax.ShapeDtypeStruct((2 * GRID, 32, EMBED), BF16),
        ),
        in_specs=[hbm] * 9,
        out_specs=(hbm, hbm, hbm),
        scratch_shapes=[
            pltpu.VMEM((ROWS, WIDTH), BF16),
            pltpu.VMEM((ROWS, EMBED), BF16),
            pltpu.VMEM((ROWS, EMBED), BF16),
            pltpu.VMEM((1, ROWS), jnp.int32),
            pltpu.VMEM((1, ROWS), jnp.int32),
            pltpu.SMEM((1,), jnp.int32),
            pltpu.VMEM((8, WIDTH, 256), BF16),
            pltpu.VMEM((4, WIDTH, 256), BF16),
            pltpu.VMEM((WIDTH, WIDTH), BF16),
            pltpu.VMEM((WIDTH, WIDTH), BF16),
            pltpu.VMEM((WIDTH, EMBED), BF16),
            pltpu.VMEM((ROWS, WIDTH), BF16),
            pltpu.VMEM((SEQ, 2, ROWS, HEAD), BF16),
            pltpu.VMEM((SEQ, 2, ROWS, HEAD), BF16),
            pltpu.VMEM((SEQ, ROWS, HEAD), BF16),
            pltpu.VMEM((SEQ, ROWS, HEAD), BF16),
            pltpu.VMEM((SEQ, ROWS, HEAD), BF16),
            pltpu.VMEM((SEQ, ROWS, HEAD), BF16),
            pltpu.VMEM((ROWS, WIDTH), BF16),
            pltpu.VMEM((POOL, ROWS, EMBED), BF16),
            pltpu.VMEM((EMBED, POOL * ROWS), BF16),
            pltpu.VMEM((POOL, 1, ROWS), jnp.int32),
            pltpu.VMEM((POOL, ROWS, ROWS), F32),
            pltpu.VMEM((POOL, ROWS, HALF), F32),
            pltpu.VMEM((POOL * ROWS, ROWS), BF16),
            pltpu.VMEM((ROWS, WIDTH), BF16),
            pltpu.VMEM((ROWS, EMBED), BF16),
            pltpu.VMEM((ROWS, EMBED), BF16),
            pltpu.VMEM((EMBED, ROWS), F32),
            pltpu.VMEM((ROWS, EMBED), F32),
            pltpu.VMEM((8, ROWS, EMBED), BF16),
            pltpu.VMEM((8, ROWS, EMBED), BF16),
            pltpu.VMEM((8, ROWS, EMBED), F32),
            pltpu.VMEM((4, 128, EMBED), BF16),
            pltpu.VMEM((4, 128, EMBED), BF16),
            pltpu.VMEM((4, 128, EMBED), BF16),
            pltpu.VMEM((4, 128, EMBED), BF16),
            pltpu.VMEM((4, 2, 128, EMBED), BF16),
            pltpu.VMEM((4, 2, 128, EMBED), BF16),
            pltpu.VMEM((128, EMBED), BF16),
            pltpu.VMEM((128, EMBED), BF16),
            pltpu.VMEM((EMBED, ROWS), F32),
            pltpu.VMEM((2, SEQ, 32, HALF), BF16),
            pltpu.VMEM((2, SEQ, 32, HALF), BF16),
            pltpu.VMEM((WIDTH // 2, EMBED), F32),
            pltpu.VMEM((WIDTH // 2, EMBED), BF16),
            pltpu.VMEM((WIDTH // 2, EMBED), BF16),
            pltpu.VMEM((WIDTH // 2, EMBED), BF16),
            pltpu.VMEM((GRID, 32, EMBED), BF16),
            pltpu.VMEM((SEQ, 32, EMBED), BF16),
            pltpu.VMEM((2 * GRID, 32, EMBED), BF16),
            pltpu.VMEM((1, ROWS), F32),
            pltpu.VMEM((EMBED // SEQ, ROWS), F32),
            dma((33,)),
            dma((2, SEQ)),
            dma((2, SEQ)),
            dma((2, 2, SEQ)),
            dma((2, POOL)),
            dma((2, POOL)),
            dma((2, 8)),
            dma((2, 4)),
            dma((2, 4)),
            dma((2, 4)),
            dma((2,)),
            dma((2, 2, SEQ)),
            dma((2,)),
            dma((2, GRID)),
            dma((2, SEQ)),
            dma((2, GRID)),
            dma((2,)),
            dma((4,)),
        ],
        compiler_params=pltpu.CompilerParams(
            collective_id=0, has_side_effects=True, vmem_limit_bytes=56 * 1024 * 1024
        ),
    )(
        tokens[0],
        w_in,
        w_out,
        w_proj,
        pos_embed[0],
        pos_ids,
        lengths,
        neg_embed[0],
        neg_ids,
    )
    loss, dneg_t, dproj = pl.pallas_call(
        finish,
        out_shape=(
            jax.ShapeDtypeStruct((1, ROWS), F32),
            jax.ShapeDtypeStruct((EMBED // SEQ, ROWS), F32),
            jax.ShapeDtypeStruct((WIDTH, EMBED), F32),
        ),
        in_specs=[hbm] * 3,
        out_specs=(hbm, hbm, hbm),
        scratch_shapes=[
            pltpu.VMEM((4, WIDTH // 4, EMBED), BF16),
            pltpu.VMEM((4, WIDTH // 4, EMBED), F32),
            dma((10,)),
        ],
    )(loss, dneg_t, dproj.reshape(WIDTH, EMBED))
    return (loss, jnp.transpose(dneg_t)[None], dproj)


def solution(mesh):
    placed = (
        P(("batch", "pool"), "seq", None),
        P(),
        P(),
        P(),
        P(("batch", "pool"), "seq", None),
        P(("batch", "pool"), "seq"),
        P(("batch", "pool")),
        P("batch", "pool", None),
        P("batch", "pool"),
    )
    return jax.shard_map(
        body,
        mesh=mesh,
        in_specs=placed,
        out_specs=(P(("batch", "pool"), "seq"), P("batch", "pool", "seq"), P()),
        check_vma=False,
    )
```
